32 devices in a mesh: cycle: 8 (over z, core), bin: 4 (over y, x).
Axes of the slice: x: 2, y: 2, z: 4, core: 2. Of those that a mesh axis runs over, the one named last changes fastest.
Arguments:
- obs_minus_bg: bfloat16 [16384, 640], P(('cycle', 'bin')), may hold values from -30 to 30, as said below
- obs_minus_an: bfloat16 [16384, 640], P(('cycle', 'bin')), may hold values from -30 to 30, as said below
- tile_of_row: int32 [16384, 1], P(('cycle', 'bin')), may hold values from 0 to 11; in each aligned block of 512 rows (0 to 511, 512 to 1023, ...) at most 85 rows name the same one
- owner_order: int32 [12], replicated, may hold values from 0 to 11, as said below
Outputs:
- error_cov: float32 [12, 640, 640], P('bin', 'cycle')
The draws below stay inside these ranges and needn't reach their ends.
Inputs may be any that keep to these rules, and one draw needn't show every extreme that they name: `obs_minus_bg`: each row's value lies in this range. `obs_minus_an`: each row's value lies in this range. `tile_of_row`: the rows of one device name one tile at most 85 times; some tile reaches it; every tile is named by some row. `owner_order`: a permutation of the tiles in which entry b * 3 + i is a tile of instrument i, so each index of bin owns one scan bin of each instrument.
All inputs are finite; a program needn't handle non-finite values.
Results may differ from the reference program's by a relative error of at most 0.0003.
Values may be sent and summed in bfloat16 or wider, within the bound.
No kernel may reach another device: no remote copies, remote signals or barrier semaphores. Data moves between devices by JAX's collectives and lax.ppermute only.
A program may use at most 320 MiB of HBM per device.

```python
import math
import jax
import jax.numpy as jnp
import numpy as np
from jax import lax

F = 640
C_IASI = 616
C_CRIS = 431
C_ATMS = 22
ROWS_DEV = 512
NTILES = 12
NSCAN = 4
MOSTT = 85
ROWS = 16384
N_CYCLE = 8
N_BIN = 4


def departures(key):
    base = jax.random.fold_in(key, 11)
    key_bias, key_scale, key_noise, key_extra = jax.random.split(base, 4)
    bias = jax.random.uniform(key_bias, (1, F), jnp.float32, -1.0, 1.0)
    scale = jnp.exp(jax.random.uniform(key_scale, (ROWS, 1), jnp.float32, jnp.log(0.5), jnp.log(5.0)))
    noise = jax.random.normal(key_noise, (ROWS, F), jnp.float32)
    first = jnp.clip(bias + scale * noise, -30.0, 30.0)
    second = jnp.clip(0.6 * first + 0.5 * jax.random.normal(key_extra, (ROWS, F), jnp.float32), -30.0, 30.0)
    return (first, second)


def draw_obs_minus_bg(key, part):
    first, second = departures(key)
    return first.astype(jnp.bfloat16)


def draw_obs_minus_an(key, part):
    first, second = departures(key)
    return second.astype(jnp.bfloat16)


def draw_owner_order(key, part):
    base = jax.random.fold_in(key, 23)
    columns = []
    for instrument in range(3):
        shuffled = jax.random.permutation(jax.random.fold_in(base, instrument), NSCAN).astype(jnp.int32)
        columns.append(shuffled + instrument * NSCAN)
    return jnp.stack(columns, axis=1).reshape(-1).astype(jnp.int32)


def deal_out(own_key, own, number, rows, number_of, top, reach, skew):
    order = jax.random.permutation(own_key, number_of)
    packed, ordinary = portions_of(number_of, rows * top, reach, skew, True), portions_of(number_of, rows * top, reach, skew, False)
    places = jnp.arange(number_of)

    def named(tallies, rotation):
        used = int((tallies > 0).sum())
        fixed = max(1, used // 4)
        shifted = fixed + (places - fixed + rotation * (used - fixed)) % max(1, number_of - fixed)
        return jnp.zeros((number_of,), jnp.int32).at[order[jnp.where(places < fixed, places, shifted)]].set(jnp.asarray(tallies, jnp.int32))

    tallies = jnp.where(number % 4 == 0, named(packed, number // 4), named(ordinary, number - number // 4 - 1))
    mixed = jax.random.permutation(jax.random.fold_in(own, 3), number_of)
    giver, taker = mixed[0:number_of // 2 * 2:2], mixed[1:number_of // 2 * 2:2]
    slack = jnp.minimum(tallies[giver] - 1, reach - tallies[taker]) // 2
    slack = jnp.where((giver == order[0]) | (taker == order[0]) | (tallies[taker] == 0), 0, jnp.maximum(slack, 0))
    shifted = jax.random.randint(jax.random.fold_in(own, 4), (number_of // 2,), 0, 1 << 20) % (slack + 1)
    tallies = tallies.at[giver].add(-shifted).at[taker].add(shifted)
    members = jnp.searchsorted(jnp.cumsum(tallies), jnp.arange(rows * top), side="right").astype(jnp.int32)
    table = members.reshape(top, rows).T
    table = table[jax.random.permutation(jax.random.fold_in(own, 1), rows)]
    rotation = jax.random.randint(jax.random.fold_in(own, 2), (rows, 1), 0, top)
    return jnp.take_along_axis(table, (jnp.arange(top)[None, :] + rotation) % top, axis=1)


def portions_of(number_of, total, most, skew, full):
    portions = [(1 << 20) // math.isqrt(rank ** skew) + 1 for rank in range(1, number_of + 1)]
    largest = most if full else min(most, max(-(-total // number_of), total * portions[0] // sum(portions)))
    least = 1 if total - largest >= number_of - 1 else 0
    counts, surplus = [largest] + [least] * (number_of - 1), total - largest - least * (number_of - 1)
    while surplus > 0:
        candidates = [i for i in range(1, number_of) if counts[i] < largest] or [i for i in range(1, number_of) if counts[i] < most]
        whole, left = sum([portions[i] for i in candidates]), surplus
        for i in candidates:
            extra = min(most - counts[i], max(1, left * portions[i] // whole), surplus)
            counts[i] = counts[i] + extra
            surplus = surplus - extra
    return np.array(counts)


def setup_inputs(seed: int = 0) -> dict:
    splits = jax.random.split(jax.random.key(seed), 5)
    obs_minus_bg = draw_obs_minus_bg(jax.random.fold_in(splits[4], 71), 0)
    obs_minus_an = draw_obs_minus_an(jax.random.fold_in(splits[4], 71), 0)
    tile_of_row_keys = jax.random.split(jax.random.fold_in(splits[2], 1), ROWS // ROWS_DEV)
    tile_of_row_turns = jax.random.permutation(jax.random.fold_in(splits[2], 3), ROWS // ROWS_DEV)
    tile_of_row = jax.vmap(lambda own, number: deal_out(jax.random.fold_in(splits[2], 2), own, number, ROWS_DEV, NTILES, 1, MOSTT, 2))(tile_of_row_keys, tile_of_row_turns).reshape((ROWS, 1))
    owner_order = draw_owner_order(jax.random.fold_in(splits[4], 71), 0)
    return dict(obs_minus_bg=obs_minus_bg, obs_minus_an=obs_minus_an, tile_of_row=tile_of_row, owner_order=owner_order)


def reference(obs_minus_bg, obs_minus_an, tile_of_row, owner_order):
    tile = tile_of_row[:, 0]
    instr = tile // NSCAN
    limit = jnp.where(instr == 0, C_IASI, jnp.where(instr == 1, C_CRIS, C_ATMS))
    keep = jnp.arange(F)[None, :] < limit[:, None]
    zero = jnp.zeros((), jnp.bfloat16)
    masked_bg = jnp.where(keep, obs_minus_bg, zero)
    masked_an = jnp.where(keep, obs_minus_an, zero)
    onehot = (tile[:, None] == jnp.arange(NTILES)[None, :]).astype(jnp.int32)
    rank = jnp.sum((jnp.cumsum(onehot, axis=0) - 1) * onehot, axis=1)
    capacity = N_CYCLE * N_BIN * MOSTT
    index_table = jnp.full((NTILES * capacity,), ROWS, jnp.int32)
    index_table = index_table.at[(tile * capacity + rank).astype(jnp.int32)].set(jnp.arange(ROWS, dtype=jnp.int32))
    padded_bg = jnp.concatenate([masked_bg, jnp.zeros((1, F), jnp.bfloat16)], axis=0)
    padded_an = jnp.concatenate([masked_an, jnp.zeros((1, F), jnp.bfloat16)], axis=0)
    count = jnp.sum(onehot, axis=0).astype(jnp.float32)

    def per_tile(t):
        rows_idx = lax.dynamic_slice_in_dim(index_table, (t * capacity).astype(jnp.int32), capacity)
        block_bg = padded_bg[rows_idx]
        block_an = padded_an[rows_idx]
        cross = jnp.dot(block_bg.T, block_an, preferred_element_type=jnp.float32)
        return cross, jnp.sum(block_bg.astype(jnp.float32), axis=0), jnp.sum(block_an.astype(jnp.float32), axis=0)

    cross_sum, sum_bg, sum_an = lax.map(per_tile, jnp.arange(NTILES, dtype=jnp.int32))
    cross_sum = cross_sum[owner_order]
    mean_bg = sum_bg[owner_order] / count[owner_order][:, None]
    mean_an = sum_an[owner_order] / count[owner_order][:, None]
    return cross_sum / count[owner_order][:, None, None] - mean_bg[:, :, None] * mean_an[:, None, :]
```

```python
import functools

import jax
import jax.numpy as jnp
from jax import lax
from jax.experimental import pallas as pl
from jax.experimental.pallas import tpu as pltpu
from jax.sharding import PartitionSpec as P

C_IASI = 616
C_CRIS = 431
C_ATMS = 22
WIDE = 640
MID = 512
ATMS_AT = 448
SUMS = 8

VMEM = pl.BlockSpec(memory_space=pltpu.VMEM)
SMEM = pl.BlockSpec(memory_space=pltpu.SMEM)
PARAMS = pltpu.CompilerParams(vmem_limit_bytes=48 * 1024 * 1024)


def row_keys(order_ref, tile_ref, me, n_bin, per_owner):
    rows = tile_ref.shape[1]
    tiles = n_bin * per_owner
    padded = -(-tiles // 16) * 16
    place = lax.broadcasted_iota(jnp.int32, (padded, rows), 0)
    wanted = jnp.full((padded, rows), -1, jnp.int32)
    for k in range(n_bin):
        for i in range(per_owner):
            wanted = jnp.where(place == k * per_owner + i, order_ref[(me ^ k) * per_owner + i], wanted)
    hits = wanted == tile_ref[...]
    before = lax.broadcasted_iota(jnp.int32, (rows, rows), 0) < lax.broadcasted_iota(jnp.int32, (rows, rows), 1)
    rank = jnp.dot(
        hits.astype(jnp.float32).astype(jnp.bfloat16),
        before.astype(jnp.float32).astype(jnp.bfloat16),
        preferred_element_type=jnp.float32,
    )
    return jnp.where(hits, rank, -1.0).astype(jnp.int32)


def placing(keys, instrument, n_bin, per_owner, slots):
    slot = lax.broadcasted_iota(jnp.int32, (slots, keys.shape[1]), 0)
    parts = [
        (slot == keys[k * per_owner + instrument : k * per_owner + instrument + 1, :]).astype(jnp.float32)
        for k in range(n_bin)
    ]
    return jnp.concatenate(parts, axis=0).astype(jnp.bfloat16)


def marked(values, limit, one_at):
    lane = lax.broadcasted_iota(jnp.int32, values.shape, 1)
    ones = jnp.where(lane == one_at, 1.0, 0.0)
    return jnp.where(lane < limit, values.astype(jnp.float32), ones).astype(jnp.bfloat16)


def place_wide_kernel(n_bin, per_owner, slots, order_ref, tile_ref, bg_ref, an_ref, *out_refs):
    me = lax.axis_index("bin")
    keys = row_keys(order_ref, tile_ref, me, n_bin, per_owner)
    select = placing(keys, 0, n_bin, per_owner, slots)
    for part, ref in enumerate((bg_ref, an_ref)):
        values = marked(ref[:, :WIDE], C_IASI, WIDE - 1)
        placed = jnp.dot(select, values, preferred_element_type=jnp.float32)
        for k in range(n_bin):
            out_refs[k][:, part * WIDE : (part + 1) * WIDE] = placed[k * slots : (k + 1) * slots].astype(jnp.bfloat16)


def place_mid_kernel(n_bin, per_owner, slots, order_ref, tile_ref, bg_ref, an_ref, *out_refs):
    me = lax.axis_index("bin")
    keys = row_keys(order_ref, tile_ref, me, n_bin, per_owner)
    select_cris = placing(keys, 1, n_bin, per_owner, slots)
    select_atms = placing(keys, 2, n_bin, per_owner, slots)
    shift = ATMS_AT % 128
    for part, ref in enumerate((bg_ref, an_ref)):
        cris = marked(ref[:, :MID], C_CRIS, MID - 1)
        atms = marked(ref[:, :128], C_ATMS, 126 - shift)
        placed = jnp.dot(select_cris, cris, preferred_element_type=jnp.float32)
        aside = jnp.dot(select_atms, atms, preferred_element_type=jnp.float32)
        placed_last = placed[:, MID - 128 :] + pltpu.roll(aside, shift, 1)
        for k in range(n_bin):
            at = slice(k * slots, (k + 1) * slots)
            out_refs[k][:, part * MID : (part + 1) * MID - 128] = placed[at, : MID - 128].astype(jnp.bfloat16)
            out_refs[k][:, (part + 1) * MID - 128 : (part + 1) * MID] = placed_last[at].astype(jnp.bfloat16)


def chunk_order(z):
    return (3 - 3 * (z % 2), 2 - z // 2, (2 * z + 1) % 5, z)


def moment_kernel(lanes, rows_c, n_cycle, n_in, *refs):
    in_refs, out_refs, cross_ref = refs[:n_in], refs[n_in:-1], refs[-1]
    cross = jnp.zeros((lanes, lanes), jnp.float32)
    for ref in in_refs:
        cross = cross + lax.dot_general(
            ref[:, :lanes], ref[:, lanes:], (((0,), (0,)), ((), ())), preferred_element_type=jnp.float32
        )
    cross_ref[:lanes, :] = cross
    if lanes == MID:
        cross_ref[lanes:, :] = jnp.zeros((cross_ref.shape[0] - lanes, lanes), jnp.float32)
        lane = lax.broadcasted_iota(jnp.int32, (24, 128), 1) + (MID - 128)
        moved = (lane >= ATMS_AT) & (lane < MID - 1)
        cross_ref[:24, MID - 128 :] = jnp.where(
            moved, cross_ref[ATMS_AT : ATMS_AT + 24, MID - 128 :], cross_ref[:24, MID - 128 :]
        )
    sums = cross_ref[lanes - SUMS : lanes, :]
    if len(out_refs) == 2:
        cycle = lax.axis_index("cycle")
        z, core = cycle // 2, cycle % 2
        for place, chip in enumerate(chunk_order(z)):
            for out_ref, c in zip(out_refs, (chip * 2 + core, chip * 2 + 1 - core)):
                out_ref[place, :rows_c, :] = cross_ref[pl.ds(pl.multiple_of(c * rows_c, 8), rows_c), :]
                out_ref[place, rows_c:, :] = sums
    else:
        for c in range(n_cycle):
            out_refs[0][c, :rows_c, :] = cross_ref[c * rows_c : (c + 1) * rows_c, :]
            out_refs[0][c, rows_c:, :] = sums


def finish_kernel(rows_c, wide_ref, mid_ref, out_ref):
    row = lax.broadcasted_iota(jnp.int32, (rows_c, WIDE), 0) + lax.axis_index("cycle") * rows_c
    lane = lax.broadcasted_iota(jnp.int32, (rows_c, WIDE), 1)
    last = rows_c + SUMS - 1
    n = wide_ref[last:, WIDE - 1 :]
    mean_bg = wide_ref[:rows_c, WIDE - 1 :] / n
    mean_an = wide_ref[last:, :] / n
    cov = wide_ref[:rows_c, :] / n - mean_bg * mean_an
    out_ref[0] = jnp.where((lane < C_IASI) & (row < C_IASI), cov, 0.0)

    n = mid_ref[last:, MID - 1 :]
    mean_bg = mid_ref[:rows_c, MID - 1 :] / n
    mean_an = mid_ref[last:, :] / n
    cov = mid_ref[:rows_c, :] / n - mean_bg * mean_an
    out_ref[1, :, :MID] = jnp.where((lane < C_CRIS) & (row < C_CRIS), jnp.pad(cov, ((0, 0), (0, WIDE - MID))), 0.0)[:, :MID]
    out_ref[1, :, MID:] = jnp.zeros((rows_c, WIDE - MID), jnp.float32)

    n = mid_ref[last - 1 : last, MID - 2 : MID - 1]
    shift = 128 - ATMS_AT % 128
    mean_bg = mid_ref[:rows_c, MID - 2 : MID - 1] / n
    mean_an = mid_ref[last - 1 : last, MID - 128 :] / n
    cov = pltpu.roll(mid_ref[:rows_c, MID - 128 :] / n - mean_bg * mean_an, shift, 1)
    out_ref[2, :, :128] = jnp.where((lane[:, :128] < C_ATMS) & (row[:, :128] < C_ATMS), cov, 0.0)
    out_ref[2, :, 128:] = jnp.zeros((rows_c, WIDE - 128), jnp.float32)


def to_owners(parts):
    n_bin = len(parts)
    return [parts[0]] + [
        lax.ppermute(parts[k], "bin", [(i, i ^ k) for i in range(n_bin)]) for k in range(1, n_bin)
    ]


def along(pairs):
    return [(2 * a + core, 2 * b + core) for a, b in pairs for core in range(2)]


def scatter_line(mine, other):
    here = [
        mine[p] + lax.ppermute(other[p], "cycle", [(i, i ^ 1) for i in range(8)]) for p in range(4)
    ]
    z = lax.axis_index("cycle") // 2
    outer = (z == 0) | (z == 3)
    r1 = lax.ppermute(here[0], "cycle", along([(0, 1), (1, 0), (2, 3), (3, 2)]))
    r2 = lax.ppermute(here[1], "cycle", along([(0, 1), (3, 2)]))
    r3 = lax.ppermute(here[2], "cycle", along([(0, 1), (3, 2)]))
    r5 = lax.ppermute(here[2] + r1, "cycle", along([(1, 3), (2, 0)]))
    r6 = lax.ppermute(here[1] + r2, "cycle", along([(1, 2), (2, 1)]))
    return here[3] + r3 + r5 + r6 + jnp.where(outer, r1, 0.0)


def on_device(obs_minus_bg, obs_minus_an, tile_of_row, owner_order):
    n_bin = lax.axis_size("bin")
    n_cycle = lax.axis_size("cycle")
    rows, width = obs_minus_bg.shape
    tiles = owner_order.shape[0]
    per_owner = tiles // n_bin
    slots = -(-(2 * rows // tiles) // 8) * 8
    rows_c = width // n_cycle
    tile = tile_of_row.reshape(1, rows)
    totals = []
    for lanes, place_kernel in ((MID, place_mid_kernel), (WIDE, place_wide_kernel)):
        parts = pl.pallas_call(
            functools.partial(place_kernel, n_bin, per_owner, slots),
            out_shape=[jax.ShapeDtypeStruct((slots, 2 * lanes), jnp.bfloat16)] * n_bin,
            in_specs=[SMEM, VMEM, VMEM, VMEM],
            out_specs=[VMEM] * n_bin,
            compiler_params=PARAMS,
        )(owner_order, tile, obs_minus_bg, obs_minus_an)
        parts = to_owners(parts)
        chunk = (rows_c + SUMS, lanes)
        if n_cycle == 8:
            shapes = [jax.ShapeDtypeStruct((4,) + chunk, jnp.float32)] * 2
        else:
            shapes = [jax.ShapeDtypeStruct((n_cycle,) + chunk, jnp.float32)]
        moments = pl.pallas_call(
            functools.partial(moment_kernel, lanes, rows_c, n_cycle, n_bin),
            out_shape=shapes,
            in_specs=[VMEM] * n_bin,
            out_specs=[VMEM] * len(shapes),
            scratch_shapes=[pltpu.VMEM((WIDE, lanes), jnp.float32)],
            compiler_params=PARAMS,
        )(*parts)
        if n_cycle == 8:
            totals.append(scatter_line(*moments))
        else:
            totals.append(lax.psum_scatter(moments[0], "cycle", scatter_dimension=0, tiled=False))
    return pl.pallas_call(
        functools.partial(finish_kernel, rows_c),
        out_shape=jax.ShapeDtypeStruct((per_owner, rows_c, width), jnp.float32),
        in_specs=[VMEM, VMEM],
        out_specs=VMEM,
        compiler_params=PARAMS,
    )(totals[1], totals[0])


def solution(mesh):
    return jax.shard_map(
        on_device,
        mesh=mesh,
        in_specs=(
            P(("cycle", "bin"), None),
            P(("cycle", "bin"), None),
            P(("cycle", "bin"), None),
            P(),
        ),
        out_specs=P("bin", "cycle", None),
        check_vma=False,
    )
```

```python
import functools

import jax
import jax.numpy as jnp
from jax import lax
from jax.experimental import pallas as pl
from jax.experimental.pallas import tpu as pltpu
from jax.sharding import PartitionSpec as P

C_IASI = 616
C_CRIS = 431
C_ATMS = 22
WIDE = 640
MID = 512
ATMS_AT = 448
SUMS = 8

VMEM = pl.BlockSpec(memory_space=pltpu.VMEM)
HBM = pl.BlockSpec(memory_space=pltpu.HBM)
ANY = pl.BlockSpec(memory_space=pl.ANY)
FIRST_VMEM = 62 * 1024 * 1024
PARAMS = pltpu.CompilerParams(vmem_limit_bytes=48 * 1024 * 1024)


def row_keys(order_ref, tile_ref, me, n_bin, per_owner):
    rows = tile_ref.shape[1]
    tiles = n_bin * per_owner
    padded = -(-tiles // 16) * 16
    place = lax.broadcasted_iota(jnp.int32, (padded, rows), 0)
    wanted = jnp.full((padded, rows), -1, jnp.int32)
    for k in range(n_bin):
        for i in range(per_owner):
            wanted = jnp.where(place == k * per_owner + i, order_ref[(me ^ k) * per_owner + i], wanted)
    hits = wanted == tile_ref[...]
    before = lax.broadcasted_iota(jnp.int32, (rows, rows), 0) < lax.broadcasted_iota(jnp.int32, (rows, rows), 1)
    rank = jnp.dot(
        hits.astype(jnp.float32).astype(jnp.bfloat16),
        before.astype(jnp.float32).astype(jnp.bfloat16),
        preferred_element_type=jnp.float32,
    )
    return jnp.where(hits, rank, -1.0).astype(jnp.int32)


def placing(keys, instrument, n_bin, per_owner, slots):
    slot = lax.broadcasted_iota(jnp.int32, (slots, keys.shape[1]), 0)
    parts = [
        (slot == keys[k * per_owner + instrument : k * per_owner + instrument + 1, :]).astype(jnp.float32)
        for k in range(n_bin)
    ]
    return jnp.concatenate(parts, axis=0).astype(jnp.bfloat16)


def marked(values, limit, one_at):
    lane = lax.broadcasted_iota(jnp.int32, values.shape, 1)
    ones = jnp.where(lane == one_at, 1.0, 0.0)
    return jnp.where(lane < limit, values.astype(jnp.float32), ones).astype(jnp.bfloat16)


def place_mid_kernel(n_bin, per_owner, slots, order_hbm, tile_hbm, bg_hbm, an_hbm, *refs):
    out_refs, (keys_ref, bg_ref, an_ref, order_ref, tile_ref, sem) = refs[:n_bin], refs[n_bin:]
    copies = [
        pltpu.make_async_copy(source, target, sem.at[i])
        for i, (source, target) in enumerate(
            ((order_hbm, order_ref), (tile_hbm, tile_ref), (bg_hbm, bg_ref), (an_hbm, an_ref))
        )
    ]
    for copy in copies:
        copy.start()
    copies[0].wait()
    copies[1].wait()
    keys = row_keys(order_ref, tile_ref, lax.axis_index("bin"), n_bin, per_owner)
    keys_ref[...] = keys
    select_cris, select_atms = (placing(keys, instrument, n_bin, per_owner, slots) for instrument in (1, 2))
    shift = ATMS_AT % 128
    for part, ref in enumerate((bg_ref, an_ref)):
        copies[2 + part].wait()
        cris = jnp.dot(select_cris, marked(ref[:, :MID], C_CRIS, MID - 1), preferred_element_type=jnp.float32)
        atms = jnp.dot(select_atms, marked(ref[:, :128], C_ATMS, 126 - shift), preferred_element_type=jnp.float32)
        last = pltpu.roll(atms, shift, 1) + cris[:, MID - 128 :]
        first, middle, end = part * MID, (part + 1) * MID - 128, (part + 1) * MID
        for k in range(n_bin):
            at = slice(k * slots, (k + 1) * slots)
            out_refs[k][:, first:middle] = cris[at, : MID - 128].astype(jnp.bfloat16)
            out_refs[k][:, middle:end] = last[at].astype(jnp.bfloat16)


def place_wide_kernel(n_bin, per_owner, slots, keys_ref, bg_ref, an_ref, own_ref, *refs):
    *out_refs, own_out_ref = refs
    own_out_ref[...] = own_ref[...]
    select = placing(keys_ref[...], 0, n_bin, per_owner, slots)
    for part, ref in enumerate((bg_ref, an_ref)):
        placed = jnp.dot(select, marked(ref[...], C_IASI, WIDE - 1), preferred_element_type=jnp.float32)
        for k in range(n_bin):
            out_refs[k][:, part * WIDE : (part + 1) * WIDE] = placed[k * slots : (k + 1) * slots].astype(jnp.bfloat16)


def offset_of(place, n):
    bits = n.bit_length() - 1
    return sum(1 << i for i in range(bits) if not place >> (bits - 1 - i) & 1)


def moment_kernel(lanes, rows_c, n_cycle, n_in, *refs):
    in_refs, out_refs, cross_ref = refs[:n_in], refs[n_in:-1], refs[-1]
    cross = jnp.zeros((lanes, lanes), jnp.float32)
    for ref in in_refs:
        cross = cross + lax.dot_general(
            ref[:, :lanes], ref[:, lanes:], (((0,), (0,)), ((), ())), preferred_element_type=jnp.float32
        )
    cross_ref[:lanes, :] = cross
    if lanes == MID:
        cross_ref[lanes:, :] = jnp.zeros((cross_ref.shape[0] - lanes, lanes), jnp.float32)
        lane = lax.broadcasted_iota(jnp.int32, (24, 128), 1) + (MID - 128)
        moved = (lane >= ATMS_AT) & (lane < MID - 1)
        cross_ref[:24, MID - 128 :] = jnp.where(
            moved, cross_ref[ATMS_AT : ATMS_AT + 24, MID - 128 :], cross_ref[:24, MID - 128 :]
        )
    sums = cross_ref[lanes - SUMS : lanes, :]
    me = lax.axis_index("cycle")
    chunk = rows_c + SUMS
    spans = []
    for out_ref in out_refs:
        start = spans[-1][2] if spans else 0
        spans.append((out_ref, start, start + out_ref.shape[0]))
    for place in range(n_cycle):
        c = me ^ offset_of(place, n_cycle)
        first = pl.multiple_of(c * rows_c, 8)
        for out_ref, start, end in spans:
            low, high = max(start, place * chunk), min(end, place * chunk + rows_c)
            if low < high:
                out_ref[low - start : high - start, :] = cross_ref[pl.ds(first + (low - place * chunk), high - low), :]
            if start <= place * chunk + rows_c < end:
                at = place * chunk + rows_c - start
                out_ref[at : at + SUMS, :] = sums


def finish_kernel(rows_c, wide_a_ref, wide_b_ref, mid_a_ref, mid_b_ref, out_ref):
    row = lax.broadcasted_iota(jnp.int32, (rows_c, WIDE), 0) + lax.axis_index("cycle") * rows_c
    lane = lax.broadcasted_iota(jnp.int32, (rows_c, WIDE), 1)
    last = rows_c + SUMS - 1
    total = wide_a_ref[...] + wide_b_ref[...]
    n = total[last:, WIDE - 1 :]
    cov = total[:rows_c] / n - (total[:rows_c, WIDE - 1 :] / n) * (total[last:] / n)
    out_ref[0] = jnp.where((lane < C_IASI) & (row < C_IASI), cov, 0.0)

    total = mid_a_ref[...] + mid_b_ref[...]
    n = total[last:, MID - 1 :]
    cov = total[:rows_c] / n - (total[:rows_c, MID - 1 :] / n) * (total[last:] / n)
    out_ref[1, :, :MID] = jnp.where((lane[:, :MID] < C_CRIS) & (row[:, :MID] < C_CRIS), cov, 0.0)
    out_ref[1, :, MID:] = jnp.zeros((rows_c, WIDE - MID), jnp.float32)

    n = total[last - 1 : last, MID - 2 : MID - 1]
    cov = total[:rows_c, MID - 128 :] / n - (total[:rows_c, MID - 2 : MID - 1] / n) * (total[last - 1 : last, MID - 128 :] / n)
    cov = pltpu.roll(cov, 128 - ATMS_AT % 128, 1)
    out_ref[2, :, :128] = jnp.where((lane[:, :128] < C_ATMS) & (row[:, :128] < C_ATMS), cov, 0.0)
    out_ref[2, :, 128:] = jnp.zeros((rows_c, WIDE - 128), jnp.float32)


def to_owners(parts):
    n_bin = len(parts)
    return [parts[0]] + [
        lax.ppermute(parts[k], "bin", [(i, i ^ k) for i in range(n_bin)]) for k in range(n_bin - 1, 0, -1)
    ]


def swap(value, bit, n):
    return lax.ppermute(value, "cycle", [(i, i ^ bit) for i in range(n)])


def add_kernel(near_ref, *refs):
    at = 0
    for ref in refs[:-1]:
        end = at + ref.shape[0]
        refs[-1][at:end] = near_ref[at:end] + ref[...]
        at = end


def add_after_kernel(n_after, near_ref, *refs):
    add_kernel(near_ref, *refs[: -1 - n_after], refs[-1])


def on_device(obs_minus_bg, obs_minus_an, tile_of_row, owner_order):
    n_bin = lax.axis_size("bin")
    n_cycle = lax.axis_size("cycle")
    rows, width = obs_minus_bg.shape
    tiles = owner_order.shape[0]
    per_owner = tiles // n_bin
    slots = -(-(2 * rows // tiles) // 8) * 8
    rows_c = width // n_cycle
    tile = tile_of_row.reshape(1, rows)
    padded = -(-tiles // 16) * 16
    *mid, keys, bg, an = pl.pallas_call(
        functools.partial(place_mid_kernel, n_bin, per_owner, slots),
        out_shape=[jax.ShapeDtypeStruct((slots, 2 * MID), jnp.bfloat16)] * n_bin
        + [jax.ShapeDtypeStruct((padded, rows), jnp.int32)]
        + [jax.ShapeDtypeStruct((rows, width), jnp.bfloat16)] * 2,
        in_specs=[HBM] * 4,
        out_specs=[VMEM] * (n_bin + 3),
        scratch_shapes=[
            pltpu.SMEM((tiles,), jnp.int32),
            pltpu.VMEM((1, rows), jnp.int32),
            pltpu.SemaphoreType.DMA((4,)),
        ],
        compiler_params=pltpu.CompilerParams(vmem_limit_bytes=FIRST_VMEM),
    )(owner_order, tile, obs_minus_bg, obs_minus_an)
    *wide, own = pl.pallas_call(
        functools.partial(place_wide_kernel, n_bin, per_owner, slots),
        out_shape=[jax.ShapeDtypeStruct((slots, 2 * WIDE), jnp.bfloat16)] * n_bin
        + [jax.ShapeDtypeStruct((slots, 2 * MID), jnp.bfloat16)],
        in_specs=[VMEM] * 4,
        out_specs=[VMEM] * (n_bin + 1),
        compiler_params=PARAMS,
    )(keys, bg, an, mid[0])

    eighth = n_cycle // 8 * (rows_c + SUMS)

    def moments(lanes, parts, cuts):
        sizes = list(cuts) + [eighth] * 7
        return pl.pallas_call(
            functools.partial(moment_kernel, lanes, rows_c, n_cycle, n_bin),
            out_shape=[jax.ShapeDtypeStruct((size, lanes), jnp.float32) for size in sizes],
            in_specs=[VMEM] * n_bin,
            out_specs=[VMEM] * len(sizes),
            scratch_shapes=[pltpu.VMEM((WIDE, lanes), jnp.float32)],
            compiler_params=PARAMS,
        )(*parts)

    def add(near, *terms, after=()):
        return pl.pallas_call(
            functools.partial(add_after_kernel, len(after)),
            out_shape=jax.ShapeDtypeStruct(near.shape, jnp.float32),
            in_specs=[VMEM] * (1 + len(terms)) + [ANY] * len(after),
            out_specs=VMEM,
            compiler_params=PARAMS,
        )(near, *terms, *after)

    def finer(send, keep, bit):
        while True:
            got = swap(send, bit, n_cycle)
            bit *= 2
            if bit == n_cycle:
                return keep, got
            half = keep.shape[0] // 2
            send, keep = keep[:half] + got[:half], keep[half:] + got[half:]

    mid_got = [own] + to_owners(mid)[1:]
    wide_got = to_owners(wide)
    far_a, far_b, far_c, far_d, near_a, near_b, near_c, near_d = moments(MID, mid_got, (eighth,))
    core_a, core_b, core_c, core_d = (swap(part, 1, n_cycle) for part in (far_a, far_b, far_c, far_d))
    mid_z_a = swap(add(near_a, core_a), 2, n_cycle)
    mid_z_b = swap(add(near_b, core_b), 2, n_cycle)
    mid_send = add(add(near_c, core_c), mid_z_a)
    mid_total = finer(mid_send, add(add(near_d, core_d), mid_z_b), 4)

    cut = eighth * 8 // 11 // 8 * 8
    far_a, far_a2, far_b, far_c, far_d, near_a, near_b, near_c, near_d = moments(
        WIDE, wide_got, (cut, eighth - cut)
    )
    core_a, core_a2, core_b, core_c, core_d = (
        swap(part, 1, n_cycle) for part in (far_a, far_a2, far_b, far_c, far_d)
    )
    wide_z_a = swap(add(near_a, core_a, core_a2, after=(mid_z_a, mid_z_b)), 2, n_cycle)
    wide_z_b = swap(add(near_b, core_b), 2, n_cycle)
    wide_send = add(add(near_c, core_c), wide_z_a, after=mid_total[1:])
    wide_keep = add(add(near_d, core_d), wide_z_b)
    wide_total = finer(wide_send, wide_keep, 4)
    return pl.pallas_call(
        functools.partial(finish_kernel, rows_c),
        out_shape=jax.ShapeDtypeStruct((per_owner, rows_c, width), jnp.float32),
        in_specs=[VMEM] * 4,
        out_specs=VMEM,
        compiler_params=PARAMS,
    )(*wide_total, *mid_total)


def solution(mesh):
    return jax.shard_map(
        on_device,
        mesh=mesh,
        in_specs=(
            P(("cycle", "bin"), None),
            P(("cycle", "bin"), None),
            P(("cycle", "bin"), None),
            P(),
        ),
        out_specs=P("bin", "cycle", None),
        check_vma=False,
    )
```

```python
import functools

import jax
import jax.numpy as jnp
from jax import lax
from jax.experimental import pallas as pl
from jax.experimental.pallas import tpu as pltpu
from jax.sharding import PartitionSpec as P

C_IASI = 616
C_CRIS = 431
C_ATMS = 22
WIDE = 640
ATMS_AT = 616
MID = 512
CRIS_ONE = 431
CRIS_AN = 432
CRIS_COLUMNS = 384
CRIS_SLOT = CRIS_COLUMNS + MID
SUMS = 8

VMEM = pl.BlockSpec(memory_space=pltpu.VMEM)
HBM = pl.BlockSpec(memory_space=pltpu.HBM)
ANY = pl.BlockSpec(memory_space=pl.ANY)
PARAMS = pltpu.CompilerParams(vmem_limit_bytes=48 * 1024 * 1024)


CFG = {'first': 'M', 'order': {'F': (3, 2, 1), 'S': (1, 3, 2)}, 'core': {'F': (48, 88, 168), 'S': (64, 128, 144, 168, 208, 216)}, 'z1': {'F': (88, 128), 'S': (88,)}, 'z2': {'F': (), 'S': (40,)}, 'after': {('z1', 'S', 0): (('z1', 'F', 0),), ('z1', 'F', 2): (('z2', 'F', 0),), ('keep', 'F'): (('z1', 'F', 0),)}}


def row_keys(order_ref, tile_ref, me, n_bin, per_owner):
    rows = tile_ref.shape[1]
    tiles = n_bin * per_owner
    padded = -(-tiles // 16) * 16
    place = lax.broadcasted_iota(jnp.int32, (padded, rows), 0)
    wanted = jnp.full((padded, rows), -1, jnp.int32)
    for k in range(n_bin):
        for i in range(per_owner):
            wanted = jnp.where(place == k * per_owner + i, order_ref[(me ^ k) * per_owner + i], wanted)
    hits = wanted == tile_ref[...]
    before = lax.broadcasted_iota(jnp.int32, (rows, rows), 0) < lax.broadcasted_iota(jnp.int32, (rows, rows), 1)
    rank = jnp.dot(
        hits.astype(jnp.float32).astype(jnp.bfloat16),
        before.astype(jnp.float32).astype(jnp.bfloat16),
        preferred_element_type=jnp.float32,
    )
    return jnp.where(hits, rank, -1.0).astype(jnp.int32)


def placing(keys, instrument, n_bin, per_owner, slots):
    slot = lax.broadcasted_iota(jnp.int32, (slots, keys.shape[1]), 0)
    parts = [
        (slot == keys[k * per_owner + instrument : k * per_owner + instrument + 1, :]).astype(jnp.float32)
        for k in range(n_bin)
    ]
    return jnp.concatenate(parts, axis=0).astype(jnp.bfloat16)


def marked(values, limit, one_at):
    lane = lax.broadcasted_iota(jnp.int32, values.shape, 1)
    ones = jnp.where(lane == one_at, 1.0, 0.0)
    return jnp.where(lane < limit, values.astype(jnp.float32), ones).astype(jnp.bfloat16)


def place_wide(keys, out_refs, part, values, n_bin, per_owner, slots):
    iasi, atms = (placing(keys, instrument, n_bin, per_owner, slots) for instrument in (0, 2))
    placed = jnp.dot(iasi, marked(values, C_IASI, WIDE - 1), preferred_element_type=jnp.float32)
    aside = jnp.dot(atms, marked(values[:, :128], C_ATMS, C_ATMS), preferred_element_type=jnp.float32)
    last = placed[:, WIDE - 128 :] + pltpu.roll(aside, ATMS_AT % 128, 1)
    first, middle, end = part * WIDE, (part + 1) * WIDE - 128, (part + 1) * WIDE
    for k in range(n_bin):
        at = slice(k * slots, (k + 1) * slots)
        out_refs[k][:, first:middle] = placed[at, : WIDE - 128].astype(jnp.bfloat16)
        out_refs[k][:, middle:end] = last[at].astype(jnp.bfloat16)


def place_mid(keys, out_refs, part, values, n_bin, per_owner, slots):
    cris = placing(keys, 1, n_bin, per_owner, slots)
    placed = jnp.dot(cris, marked(values[:, :MID], C_CRIS, CRIS_ONE), preferred_element_type=jnp.float32)
    if part == 1:
        placed = pltpu.roll(placed, CRIS_AN - CRIS_COLUMNS, 1)
    for k in range(n_bin):
        rows = placed[k * slots : (k + 1) * slots]
        if part == 0:
            out_refs[k][:, :MID] = rows.astype(jnp.bfloat16)
        else:
            shared = out_refs[k][:, CRIS_COLUMNS:MID].astype(jnp.float32) + rows[:, : MID - CRIS_COLUMNS]
            out_refs[k][:, CRIS_COLUMNS:MID] = shared.astype(jnp.bfloat16)
            out_refs[k][:, MID:] = rows[:, MID - CRIS_COLUMNS :].astype(jnp.bfloat16)


def first_place_kernel(place, sizes, order_hbm, tile_hbm, bg_hbm, an_hbm, *refs):
    n_bin = sizes[0]
    out_refs, (keys_ref, bg_ref, an_ref, order_ref, tile_ref, sem) = refs[:n_bin], refs[n_bin:]
    copies = [
        pltpu.make_async_copy(source, target, sem.at[i])
        for i, (source, target) in enumerate(
            ((order_hbm, order_ref), (tile_hbm, tile_ref), (bg_hbm, bg_ref), (an_hbm, an_ref))
        )
    ]
    for copy in copies:
        copy.start()
    copies[0].wait()
    copies[1].wait()
    keys = row_keys(order_ref, tile_ref, lax.axis_index("bin"), *sizes[:2])
    keys_ref[...] = keys
    for part, ref in enumerate((bg_ref, an_ref)):
        copies[2 + part].wait()
        place(keys, out_refs, part, ref[...], *sizes)


def second_place_kernel(place, sizes, keys_ref, bg_ref, an_ref, *out_refs):
    for part, ref in enumerate((bg_ref, an_ref)):
        place(keys_ref[...], out_refs, part, ref[...], *sizes)


def offset_of(place, n):
    bits = n.bit_length() - 1
    return sum(1 << i for i in range(bits) if not place >> (bits - 1 - i) & 1)


def moment_kernel(lanes, rows_c, n_cycle, n_in, n_after, *refs):
    in_refs, out_refs, cross_ref = refs[:n_in], refs[n_in + n_after : -1], refs[-1]
    columns, sums_end = (WIDE, WIDE) if lanes == WIDE else (CRIS_COLUMNS, CRIS_ONE + 1)
    cross = jnp.zeros((lanes, lanes), jnp.float32)
    for ref in in_refs:
        cross = cross + lax.dot_general(
            ref[:, :lanes],
            ref[:, columns : columns + lanes],
            (((0,), (0,)), ((), ())),
            preferred_element_type=jnp.float32,
        )
    cross_ref[:lanes, :] = cross
    if lanes == WIDE:
        lane = lax.broadcasted_iota(jnp.int32, (WIDE - ATMS_AT, 128), 1) + (WIDE - 128)
        cross_ref[: WIDE - ATMS_AT, WIDE - 128 :] = jnp.where(
            (lane >= ATMS_AT) & (lane < WIDE - 1),
            cross_ref[ATMS_AT:, WIDE - 128 :],
            cross_ref[: WIDE - ATMS_AT, WIDE - 128 :],
        )
    else:
        cross_ref[lanes:, :] = jnp.zeros((cross_ref.shape[0] - lanes, lanes), jnp.float32)
    sums = cross_ref[sums_end - SUMS : sums_end, :]
    me = lax.axis_index("cycle")
    segments, end = [], 0
    for place in range(n_cycle):
        segments.append((place, end, end + rows_c))
        end += rows_c
        if place % (n_cycle // 4) == n_cycle // 8 - 1:
            segments.append((None, end, end + SUMS))
            end += SUMS
    start = 0
    for out_ref in out_refs:
        end = start + out_ref.shape[0]
        for place, first, last in segments:
            low, high = max(start, first), min(end, last)
            if low < high:
                if place is None:
                    rows = sums[low - first : high - first]
                else:
                    row = (me ^ offset_of(place, n_cycle)) * rows_c + (low - first)
                    rows = cross_ref[pl.ds(pl.multiple_of(row, 8), high - low), :]
                out_ref[low - start : high - start, :] = rows
        start = end


def finish_kernel(rows_c, n_wide, n_mid, *refs):
    wide_keep_ref, wide_send_ref, *wide_got = refs[: 2 + n_wide]
    mid_keep_ref, mid_send_ref, *mid_got = refs[2 + n_wide : -1]
    out_ref = refs[-1]
    wide_got = jnp.concatenate([ref[...] for ref in wide_got])
    mid_got = jnp.concatenate([ref[...] for ref in mid_got])
    row = lax.broadcasted_iota(jnp.int32, (rows_c, WIDE), 0) + lax.axis_index("cycle") * rows_c
    lane = lax.broadcasted_iota(jnp.int32, (rows_c, WIDE), 1)
    total = wide_keep_ref[...] + wide_got[:rows_c]
    sums = wide_send_ref[wide_send_ref.shape[0] - SUMS :] + wide_got[rows_c:]

    def covariance(total, one, sums):
        n = sums[:, one : one + 1]
        return total / n - (total[:, one : one + 1] / n) * (sums / n)

    cov = covariance(total, WIDE - 1, sums[SUMS - 1 :])
    out_ref[0] = jnp.where((lane < C_IASI) & (row < C_IASI), cov, 0.0)
    cov = covariance(total[:, WIDE - 128 :], 126, sums[SUMS - 2 : SUMS - 1, WIDE - 128 :])
    cov = pltpu.roll(cov, 128 - ATMS_AT % 128, 1)
    out_ref[2, :, :128] = jnp.where((lane[:, :128] < C_ATMS) & (row[:, :128] < C_ATMS), cov, 0.0)
    out_ref[2, :, 128:] = jnp.zeros((rows_c, WIDE - 128), jnp.float32)

    total = mid_keep_ref[...] + mid_got[:rows_c]
    sums = mid_send_ref[mid_send_ref.shape[0] - SUMS :] + mid_got[rows_c:]
    cov = covariance(total, CRIS_AN - CRIS_COLUMNS + CRIS_ONE, sums[SUMS - 1 :])
    cov = pltpu.roll(cov, MID - (CRIS_AN - CRIS_COLUMNS), 1)
    out_ref[1, :, :MID] = jnp.where((lane[:, :MID] < C_CRIS) & (row[:, :MID] < C_CRIS), cov, 0.0)
    out_ref[1, :, MID:] = jnp.zeros((rows_c, WIDE - MID), jnp.float32)


def to_owners(parts, order):
    n_bin = len(parts)
    return [parts[0]] + [
        lax.ppermute(parts[k], "bin", [(i, i ^ k) for i in range(n_bin)])
        for k in (order if n_bin == 4 else range(n_bin - 1, 0, -1))
    ]


def swap(value, bit, n):
    return lax.ppermute(value, "cycle", [(i, i ^ bit) for i in range(n)])


def sum_kernel(first, spans, n_after, near_ref, *refs):
    out_ref = refs[-1]
    rows = out_ref.shape[0]
    out_ref[...] = near_ref[first : first + rows]
    for ref, start in zip(refs[: len(spans)], spans):
        low, high = max(first, start), min(first + rows, start + ref.shape[0])
        out_ref[low - first : high - first] += ref[low - start : high - start]


def on_device(obs_minus_bg, obs_minus_an, tile_of_row, owner_order):
    n_bin = lax.axis_size("bin")
    n_cycle = lax.axis_size("cycle")
    rows, width = obs_minus_bg.shape
    tiles = owner_order.shape[0]
    per_owner = tiles // n_bin
    slots = -(-(2 * rows // tiles) // 8) * 8
    rows_c = width // n_cycle
    tile = tile_of_row.reshape(1, rows)
    padded = -(-tiles // 16) * 16
    sizes = (n_bin, per_owner, slots)
    cfg = CFG
    lanes = {"F": MID, "S": WIDE} if cfg["first"] == "M" else {"F": WIDE, "S": MID}
    places = {MID: place_mid, WIDE: place_wide}

    def slot_shapes(p):
        return [jax.ShapeDtypeStruct((slots, 2 * WIDE if lanes[p] == WIDE else CRIS_SLOT), jnp.bfloat16)] * n_bin

    *first, keys, bg, an = pl.pallas_call(
        functools.partial(first_place_kernel, places[lanes["F"]], sizes),
        out_shape=slot_shapes("F")
        + [jax.ShapeDtypeStruct((padded, rows), jnp.int32)]
        + [jax.ShapeDtypeStruct((rows, width), jnp.bfloat16)] * 2,
        in_specs=[HBM] * 4,
        out_specs=[VMEM] * (n_bin + 3),
        scratch_shapes=[
            pltpu.SMEM((tiles,), jnp.int32),
            pltpu.VMEM((1, rows), jnp.int32),
            pltpu.SemaphoreType.DMA((4,)),
        ],
        compiler_params=PARAMS,
    )(*(pltpu.with_memory_space_constraint(x, pltpu.HBM) for x in (owner_order, tile, obs_minus_bg, obs_minus_an)))
    second = pl.pallas_call(
        functools.partial(second_place_kernel, places[lanes["S"]], sizes),
        out_shape=slot_shapes("S"),
        in_specs=[VMEM] * 3,
        out_specs=[VMEM] * n_bin,
        compiler_params=PARAMS,
    )(keys, bg, an)
    owned = {"F": to_owners(first, cfg["order"]["F"]), "S": to_owners(second, cfg["order"]["S"])}

    kept = n_cycle // 8 * rows_c
    sent = kept + SUMS
    half = 2 * (sent + kept)

    def bounds(cuts, end):
        return list(zip([0, *cuts], [*cuts, end]))

    core_spans = {p: bounds(cfg["core"][p], half) for p in "FS"}
    z1_spans = {p: bounds(cfg["z1"][p], sent + kept) for p in "FS"}
    z2_spans = {p: bounds(cfg["z2"][p], sent) for p in "FS"}
    memo, busy = {}, set()

    def get(name):
        if name not in memo:
            assert name not in busy
            busy.add(name)
            memo[name] = make(*name)
            busy.discard(name)
        return memo[name]

    def after(*name):
        return [get(n) for n in cfg["after"].get(name, ())]

    def overlapping(kind, p, spans, low, high, shift=0):
        hits = [(i, start + shift) for i, (start, end) in enumerate(spans) if start + shift < high and low < end + shift]
        return [get((kind, p, i)) for i, _ in hits], [start for _, start in hits]

    def summed(p, low, high, z1, waits):
        terms, starts = overlapping("core", p, core_spans[p], low, high)
        if z1:
            more, more_starts = overlapping("z1", p, z1_spans[p], low, high, sent + kept)
            terms, starts = terms + more, starts + more_starts
        return pl.pallas_call(
            functools.partial(sum_kernel, low, starts, len(waits)),
            out_shape=jax.ShapeDtypeStruct((high - low, lanes[p]), jnp.float32),
            in_specs=[VMEM] * (1 + len(terms)) + [ANY] * len(waits),
            out_specs=VMEM,
            compiler_params=PARAMS,
        )(get(("moments", p))[-1], *terms, *waits)

    def make(kind, p, i=None):
        if kind == "moments":
            waits = after(kind, p)
            shapes = [end - start for start, end in core_spans[p]] + [half]
            return pl.pallas_call(
                functools.partial(moment_kernel, lanes[p], rows_c, n_cycle, n_bin, len(waits)),
                out_shape=[jax.ShapeDtypeStruct((size, lanes[p]), jnp.float32) for size in shapes],
                in_specs=[VMEM] * n_bin + [ANY] * len(waits),
                out_specs=[VMEM] * len(shapes),
                scratch_shapes=[pltpu.VMEM((WIDE, lanes[p]), jnp.float32)],
                compiler_params=PARAMS,
            )(*owned[p], *waits)
        if kind == "got":
            return owned[p][i]
        if kind == "core":
            return swap(get(("moments", p))[i], 1, n_cycle)
        if kind == "z1":
            low, high = z1_spans[p][i]
            return swap(summed(p, low, high, False, after(kind, p, i)), 2, n_cycle)
        if kind == "send":
            low, high = z2_spans[p][i]
            return summed(p, low + sent + kept, high + sent + kept, True, after(kind, p, i))
        if kind == "z2":
            return swap(get(("send", p, i)), 4, n_cycle)
        if kind == "keep":
            return summed(p, half - kept, half, True, after(kind, p))

    def ends(p):
        n = len(z2_spans[p])
        keep, send, got = get(("keep", p)), get(("send", p, n - 1)), [get(("z2", p, i)) for i in range(n)]
        bit = 8
        while bit < n_cycle:
            got = jnp.concatenate(got)
            part = keep.shape[0] // 2
            send = jnp.concatenate([keep[:part] + got[:part], send[-SUMS:] + got[-SUMS:]])
            keep, got = keep[part:] + got[part:-SUMS], [swap(send, bit, n_cycle)]
            bit *= 2
        return [keep, send, *got]

    wide, mid = (ends(p) for p in sorted("FS", key=lambda p: -lanes[p]))
    return pl.pallas_call(
        functools.partial(finish_kernel, rows_c, len(wide) - 2, len(mid) - 2),
        out_shape=jax.ShapeDtypeStruct((per_owner, rows_c, width), jnp.float32),
        in_specs=[VMEM] * (len(wide) + len(mid)),
        out_specs=VMEM,
        compiler_params=PARAMS,
    )(*wide, *mid)


def solution(mesh):
    return jax.shard_map(
        on_device,
        mesh=mesh,
        in_specs=(
            P(("cycle", "bin"), None),
            P(("cycle", "bin"), None),
            P(("cycle", "bin"), None),
            P(),
        ),
        out_specs=P("bin", "cycle", None),
        check_vma=False,
    )
```

```python
import functools

import jax
import jax.numpy as jnp
from jax import lax
from jax.experimental import pallas as pl
from jax.experimental.pallas import tpu as pltpu
from jax.sharding import PartitionSpec as P

C_IASI = 616
C_CRIS = 431
C_ATMS = 22
WIDE = 640
ATMS_AT = 616
MID = 512
CRIS_ONE = 431
CRIS_AN = 432
CRIS_COLUMNS = 384
CRIS_SLOT = CRIS_COLUMNS + MID
SUMS = 8

VMEM = pl.BlockSpec(memory_space=pltpu.VMEM)
HBM = pl.BlockSpec(memory_space=pltpu.HBM)
ANY = pl.BlockSpec(memory_space=pl.ANY)
PARAMS = pltpu.CompilerParams(vmem_limit_bytes=48 * 1024 * 1024)


CFG = {
    "first": "M",
    "order": {"F": (3, 2, 1), "S": (2, 1, 3)},
    "core": {"F": (88, 168), "S": (40, 136, 144, 168, 256)},
    "z1": {"F": (), "S": (88,)},
    "z2": {"F": (), "S": (48,)},
    "after": {
        ("send", "S", 1): (("z2", "F", 0), ("z1", "S", 0)),
        ("z1", "S", 1): (("got", "S", 2),),
    },
}


def row_keys(order_ref, tile_ref, me, n_bin, per_owner):
    rows = tile_ref.shape[1]
    tiles = n_bin * per_owner
    padded = -(-tiles // 16) * 16
    place = lax.broadcasted_iota(jnp.int32, (padded, rows), 0)
    wanted = jnp.full((padded, rows), -1, jnp.int32)
    for k in range(n_bin):
        for i in range(per_owner):
            wanted = jnp.where(place == k * per_owner + i, order_ref[(me ^ k) * per_owner + i], wanted)
    hits = wanted == tile_ref[...]
    block = 128
    before = lax.broadcasted_iota(jnp.int32, (block, block), 0) < lax.broadcasted_iota(jnp.int32, (block, block), 1)
    before = before.astype(jnp.float32).astype(jnp.bfloat16)
    ones = hits.astype(jnp.float32)
    ranks, seen = [], jnp.zeros((padded, 1), jnp.float32)
    for at in range(0, rows, block):
        here = ones[:, at : at + block]
        ranks.append(seen + jnp.dot(here.astype(jnp.bfloat16), before, preferred_element_type=jnp.float32))
        seen = seen + jnp.sum(here, axis=1, keepdims=True)
    rank = jnp.concatenate(ranks, axis=1)
    return jnp.where(hits, rank, -1.0).astype(jnp.int32)


def placing(keys, instrument, n_bin, per_owner, slots):
    slot = lax.broadcasted_iota(jnp.int32, (slots, keys.shape[1]), 0)
    parts = [
        (slot == keys[k * per_owner + instrument : k * per_owner + instrument + 1, :]).astype(jnp.float32)
        for k in range(n_bin)
    ]
    return jnp.concatenate(parts, axis=0).astype(jnp.bfloat16)


def marked(values, limit, one_at):
    lane = lax.broadcasted_iota(jnp.int32, values.shape, 1)
    ones = jnp.where(lane == one_at, 1.0, 0.0)
    return jnp.where(lane < limit, values.astype(jnp.float32), ones).astype(jnp.bfloat16)


def place_wide(keys, out_refs, part, values, n_bin, per_owner, slots):
    iasi, atms = (placing(keys, instrument, n_bin, per_owner, slots) for instrument in (0, 2))
    placed = jnp.dot(iasi, marked(values, C_IASI, WIDE - 1), preferred_element_type=jnp.float32)
    aside = jnp.dot(atms, marked(values[:, :128], C_ATMS, C_ATMS), preferred_element_type=jnp.float32)
    last = placed[:, WIDE - 128 :] + pltpu.roll(aside, ATMS_AT % 128, 1)
    first, middle, end = part * WIDE, (part + 1) * WIDE - 128, (part + 1) * WIDE
    for k in range(n_bin):
        at = slice(k * slots, (k + 1) * slots)
        out_refs[k][:, first:middle] = placed[at, : WIDE - 128].astype(jnp.bfloat16)
        out_refs[k][:, middle:end] = last[at].astype(jnp.bfloat16)


def place_mid(keys, out_refs, part, values, n_bin, per_owner, slots):
    cris = placing(keys, 1, n_bin, per_owner, slots)
    placed = jnp.dot(cris, marked(values[:, :MID], C_CRIS, CRIS_ONE), preferred_element_type=jnp.float32)
    if part == 1:
        placed = pltpu.roll(placed, CRIS_AN - CRIS_COLUMNS, 1)
    for k in range(n_bin):
        rows = placed[k * slots : (k + 1) * slots]
        if part == 0:
            out_refs[k][:, :MID] = rows.astype(jnp.bfloat16)
        else:
            shared = out_refs[k][:, CRIS_COLUMNS:MID].astype(jnp.float32) + rows[:, : MID - CRIS_COLUMNS]
            out_refs[k][:, CRIS_COLUMNS:MID] = shared.astype(jnp.bfloat16)
            out_refs[k][:, MID:] = rows[:, MID - CRIS_COLUMNS :].astype(jnp.bfloat16)


def first_place_kernel(place, sizes, order_hbm, tile_hbm, bg_hbm, an_hbm, *refs):
    n_bin = sizes[0]
    out_refs, (keys_ref, bg_ref, an_ref, order_ref, tile_ref, sem) = refs[:n_bin], refs[n_bin:]
    copies = [
        pltpu.make_async_copy(source, target, sem.at[i])
        for i, (source, target) in enumerate(
            ((order_hbm, order_ref), (tile_hbm, tile_ref), (bg_hbm, bg_ref), (an_hbm, an_ref))
        )
    ]
    for copy in copies:
        copy.start()
    copies[0].wait()
    copies[1].wait()
    keys = row_keys(order_ref, tile_ref, lax.axis_index("bin"), *sizes[:2])
    keys_ref[...] = keys
    for part, ref in enumerate((bg_ref, an_ref)):
        copies[2 + part].wait()
        place(keys, out_refs, part, ref[...], *sizes)


def second_place_kernel(place, sizes, keys_ref, bg_ref, an_ref, *out_refs):
    for part, ref in enumerate((bg_ref, an_ref)):
        place(keys_ref[...], out_refs, part, ref[...], *sizes)


def offset_of(place, n):
    bits = n.bit_length() - 1
    return sum(1 << i for i in range(bits) if not place >> (bits - 1 - i) & 1)


def moment_kernel(lanes, rows_c, n_cycle, n_in, n_after, *refs):
    in_refs, out_refs, cross_ref = refs[:n_in], refs[n_in + n_after : -1], refs[-1]
    columns, sums_end = (WIDE, WIDE) if lanes == WIDE else (CRIS_COLUMNS, CRIS_ONE + 1)
    whole = in_refs[0].shape[0] // 16 * 16

    def stacked(at):
        ends = [ref[whole:, at : at + lanes].astype(jnp.float32) for ref in in_refs]
        return jnp.concatenate(
            [ref[:whole, at : at + lanes] for ref in in_refs] + [jnp.concatenate(ends).astype(jnp.bfloat16)]
        )

    cross = lax.dot_general(
        stacked(0), stacked(columns), (((0,), (0,)), ((), ())), preferred_element_type=jnp.float32
    )
    cross_ref[:lanes, :] = cross
    if lanes == WIDE:
        lane = lax.broadcasted_iota(jnp.int32, (WIDE - ATMS_AT, 128), 1) + (WIDE - 128)
        cross_ref[: WIDE - ATMS_AT, WIDE - 128 :] = jnp.where(
            (lane >= ATMS_AT) & (lane < WIDE - 1),
            cross_ref[ATMS_AT:, WIDE - 128 :],
            cross_ref[: WIDE - ATMS_AT, WIDE - 128 :],
        )
    else:
        cross_ref[lanes:, :] = jnp.zeros((cross_ref.shape[0] - lanes, lanes), jnp.float32)
    sums = cross_ref[sums_end - SUMS : sums_end, :]
    me = lax.axis_index("cycle")
    segments, end = [], 0
    for place in range(n_cycle):
        segments.append((place, end, end + rows_c))
        end += rows_c
        if place % (n_cycle // 4) == n_cycle // 8 - 1:
            segments.append((None, end, end + SUMS))
            end += SUMS
    start = 0
    for out_ref in out_refs:
        end = start + out_ref.shape[0]
        for place, first, last in segments:
            low, high = max(start, first), min(end, last)
            if low < high:
                if place is None:
                    rows = sums[low - first : high - first]
                else:
                    row = (me ^ offset_of(place, n_cycle)) * rows_c + (low - first)
                    rows = cross_ref[pl.ds(pl.multiple_of(row, 8), high - low), :]
                out_ref[low - start : high - start, :] = rows
        start = end


def covariance(total, one, sums):
    scale = 1.0 / sums[:, one : one + 1]
    return total * scale - (total[:, one : one + 1] * scale) * (sums * scale)


def finish_mid_kernel(rows_c, keep_ref, send_ref, *refs):
    out_ref = refs[-1]
    got = jnp.concatenate([ref[...] for ref in refs[:-1]])
    row = lax.broadcasted_iota(jnp.int32, (rows_c, MID), 0) + lax.axis_index("cycle") * rows_c
    lane = lax.broadcasted_iota(jnp.int32, (rows_c, MID), 1)
    sums = send_ref[send_ref.shape[0] - SUMS :] + got[rows_c:]
    cov = covariance(keep_ref[...] + got[:rows_c], CRIS_AN - CRIS_COLUMNS + CRIS_ONE, sums[SUMS - 1 :])
    cov = pltpu.roll(cov, MID - (CRIS_AN - CRIS_COLUMNS), 1)
    out_ref[:, :MID] = jnp.where((lane < C_CRIS) & (row < C_CRIS), cov, 0.0)
    out_ref[:, MID:] = jnp.zeros((rows_c, WIDE - MID), jnp.float32)


def finish_kernel(rows_c, keep_ref, send_ref, *refs):
    *got_refs, mid_ref, out_ref, wide_ref, atms_ref, sem = refs
    mid_copy = pltpu.make_async_copy(mid_ref, out_ref.at[1], sem.at[1])
    mid_copy.start()
    got = jnp.concatenate([ref[...] for ref in got_refs])
    row = lax.broadcasted_iota(jnp.int32, (rows_c, WIDE), 0) + lax.axis_index("cycle") * rows_c
    lane = lax.broadcasted_iota(jnp.int32, (rows_c, WIDE), 1)
    total = keep_ref[...] + got[:rows_c]
    sums = send_ref[send_ref.shape[0] - SUMS :] + got[rows_c:]
    cov = covariance(total, WIDE - 1, sums[SUMS - 1 :])
    wide_ref[...] = jnp.where((lane < C_IASI) & (row < C_IASI), cov, 0.0)
    wide_copy = pltpu.make_async_copy(wide_ref, out_ref.at[0], sem.at[0])
    wide_copy.start()
    cov = covariance(total[:, WIDE - 128 :], 126, sums[SUMS - 2 : SUMS - 1, WIDE - 128 :])
    cov = pltpu.roll(cov, 128 - ATMS_AT % 128, 1)
    atms_ref[:, :128] = jnp.where((lane[:, :128] < C_ATMS) & (row[:, :128] < C_ATMS), cov, 0.0)
    atms_ref[:, 128:] = jnp.zeros((rows_c, WIDE - 128), jnp.float32)
    atms_copy = pltpu.make_async_copy(atms_ref, out_ref.at[2], sem.at[2])
    atms_copy.start()
    mid_copy.wait()
    wide_copy.wait()
    atms_copy.wait()


def to_owners(parts, order):
    n_bin = len(parts)
    return [parts[0]] + [
        lax.ppermute(parts[k], "bin", [(i, i ^ k) for i in range(n_bin)])
        for k in (order if n_bin == 4 else range(n_bin - 1, 0, -1))
    ]


def swap(value, bit, n):
    return lax.ppermute(value, "cycle", [(i, i ^ bit) for i in range(n)])


def sum_kernel(first, spans, n_after, near_ref, *refs):
    out_ref = refs[-1]
    rows = out_ref.shape[0]
    out_ref[...] = near_ref[first : first + rows]
    for ref, start in zip(refs[: len(spans)], spans):
        low, high = max(first, start), min(first + rows, start + ref.shape[0])
        out_ref[low - first : high - first] += ref[low - start : high - start]


def on_device(obs_minus_bg, obs_minus_an, tile_of_row, owner_order):
    n_bin = lax.axis_size("bin")
    n_cycle = lax.axis_size("cycle")
    rows, width = obs_minus_bg.shape
    tiles = owner_order.shape[0]
    per_owner = tiles // n_bin
    slots = -(-(2 * rows // tiles) // 8) * 8
    rows_c = width // n_cycle
    tile = tile_of_row.reshape(1, rows)
    padded = -(-tiles // 16) * 16
    sizes = (n_bin, per_owner, slots)
    cfg = CFG
    lanes = {"F": MID, "S": WIDE} if cfg["first"] == "M" else {"F": WIDE, "S": MID}
    places = {MID: place_mid, WIDE: place_wide}

    def slot_shapes(p):
        return [jax.ShapeDtypeStruct((slots, 2 * WIDE if lanes[p] == WIDE else CRIS_SLOT), jnp.bfloat16)] * n_bin

    *first, keys, bg, an = pl.pallas_call(
        functools.partial(first_place_kernel, places[lanes["F"]], sizes),
        out_shape=slot_shapes("F")
        + [jax.ShapeDtypeStruct((padded, rows), jnp.int32)]
        + [jax.ShapeDtypeStruct((rows, width), jnp.bfloat16)] * 2,
        in_specs=[HBM] * 4,
        out_specs=[VMEM] * (n_bin + 3),
        scratch_shapes=[
            pltpu.SMEM((tiles,), jnp.int32),
            pltpu.VMEM((1, rows), jnp.int32),
            pltpu.SemaphoreType.DMA((4,)),
        ],
        compiler_params=PARAMS,
    )(*(pltpu.with_memory_space_constraint(x, pltpu.HBM) for x in (owner_order, tile, obs_minus_bg, obs_minus_an)))
    second = pl.pallas_call(
        functools.partial(second_place_kernel, places[lanes["S"]], sizes),
        out_shape=slot_shapes("S"),
        in_specs=[VMEM] * 3,
        out_specs=[VMEM] * n_bin,
        compiler_params=PARAMS,
    )(keys, bg, an)
    owned = {"F": to_owners(first, cfg["order"]["F"]), "S": to_owners(second, cfg["order"]["S"])}

    kept = n_cycle // 8 * rows_c
    sent = kept + SUMS
    half = 2 * (sent + kept)

    def bounds(cuts, end):
        return list(zip([0, *cuts], [*cuts, end]))

    core_spans = {p: bounds(cfg["core"][p], half) for p in "FS"}
    z1_spans = {p: bounds(cfg["z1"][p], sent + kept) for p in "FS"}
    z2_spans = {p: bounds(cfg["z2"][p], sent) for p in "FS"}
    memo, busy = {}, set()

    def get(name):
        if name not in memo:
            assert name not in busy
            busy.add(name)
            memo[name] = make(*name)
            busy.discard(name)
        return memo[name]

    def after(*name):
        return [get(n) for n in cfg["after"].get(name, ())]

    def overlapping(kind, p, spans, low, high, shift=0):
        hits = [(i, start + shift) for i, (start, end) in enumerate(spans) if start + shift < high and low < end + shift]
        return [get((kind, p, i)) for i, _ in hits], [start for _, start in hits]

    def summed(p, low, high, z1, waits):
        terms, starts = overlapping("core", p, core_spans[p], low, high)
        if z1:
            more, more_starts = overlapping("z1", p, z1_spans[p], low, high, sent + kept)
            terms, starts = terms + more, starts + more_starts
        return pl.pallas_call(
            functools.partial(sum_kernel, low, starts, len(waits)),
            out_shape=jax.ShapeDtypeStruct((high - low, lanes[p]), jnp.float32),
            in_specs=[VMEM] * (1 + len(terms)) + [ANY] * len(waits),
            out_specs=VMEM,
            compiler_params=PARAMS,
        )(get(("moments", p))[-1], *terms, *waits)

    def make(kind, p, i=None):
        if kind == "moments":
            waits = after(kind, p)
            shapes = [end - start for start, end in core_spans[p]] + [half]
            return pl.pallas_call(
                functools.partial(moment_kernel, lanes[p], rows_c, n_cycle, n_bin, len(waits)),
                out_shape=[jax.ShapeDtypeStruct((size, lanes[p]), jnp.float32) for size in shapes],
                in_specs=[VMEM] * n_bin + [ANY] * len(waits),
                out_specs=[VMEM] * len(shapes),
                scratch_shapes=[pltpu.VMEM((WIDE, lanes[p]), jnp.float32)],
                compiler_params=PARAMS,
            )(*owned[p], *waits)
        if kind == "got":
            return owned[p][i]
        if kind == "core":
            return swap(get(("moments", p))[i], 1, n_cycle)
        if kind == "z1":
            low, high = z1_spans[p][i]
            return swap(summed(p, low, high, False, after(kind, p, i)), 2, n_cycle)
        if kind == "send":
            low, high = z2_spans[p][i]
            return summed(p, low + sent + kept, high + sent + kept, True, after(kind, p, i))
        if kind == "z2":
            return swap(get(("send", p, i)), 4, n_cycle)
        if kind == "keep":
            return summed(p, half - kept, half, True, after(kind, p))

    def ends(p):
        n = len(z2_spans[p])
        keep, send, got = get(("keep", p)), get(("send", p, n - 1)), [get(("z2", p, i)) for i in range(n)]
        bit = 8
        while bit < n_cycle:
            got = jnp.concatenate(got)
            part = keep.shape[0] // 2
            send = jnp.concatenate([keep[:part] + got[:part], send[-SUMS:] + got[-SUMS:]])
            keep, got = keep[part:] + got[part:-SUMS], [swap(send, bit, n_cycle)]
            bit *= 2
        return [keep, send, *got]

    wide, mid = (ends(p) for p in sorted("FS", key=lambda p: -lanes[p]))
    mid = pl.pallas_call(
        functools.partial(finish_mid_kernel, rows_c),
        out_shape=jax.ShapeDtypeStruct((rows_c, width), jnp.float32),
        in_specs=[VMEM] * len(mid),
        out_specs=VMEM,
        compiler_params=PARAMS,
    )(*mid)
    return pl.pallas_call(
        functools.partial(finish_kernel, rows_c),
        out_shape=jax.ShapeDtypeStruct((per_owner, rows_c, width), jnp.float32),
        in_specs=[VMEM] * (len(wide) + 1),
        out_specs=HBM,
        scratch_shapes=[
            pltpu.VMEM((rows_c, width), jnp.float32),
            pltpu.VMEM((rows_c, width), jnp.float32),
            pltpu.SemaphoreType.DMA((3,)),
        ],
        compiler_params=PARAMS,
    )(*wide, mid)


def solution(mesh):
    return jax.shard_map(
        on_device,
        mesh=mesh,
        in_specs=(
            P(("cycle", "bin"), None),
            P(("cycle", "bin"), None),
            P(("cycle", "bin"), None),
            P(),
        ),
        out_specs=P("bin", "cycle", None),
        check_vma=False,
    )
```

```python
import functools

import jax
import jax.numpy as jnp
from jax import lax
from jax.experimental import pallas as pl
from jax.experimental.pallas import tpu as pltpu
from jax.sharding import PartitionSpec as P

C_IASI = 616
C_CRIS = 431
C_ATMS = 22
WIDE = 640
ATMS_AT = 616
MID = 512
CRIS_ONE = 431
CRIS_AN = 432
CRIS_COLUMNS = 384
CRIS_SLOT = CRIS_COLUMNS + MID
SUMS = 8

VMEM = pl.BlockSpec(memory_space=pltpu.VMEM)
HBM = pl.BlockSpec(memory_space=pltpu.HBM)
ANY = pl.BlockSpec(memory_space=pl.ANY)
PARAMS = pltpu.CompilerParams(vmem_limit_bytes=48 * 1024 * 1024)


CFG = {
    "first": "M",
    "order": {"F": (3, 2, 1), "S": (2, 1, 3)},
    "core": {"F": (88, 168), "S": (40, 136, 144, 168, 256)},
    "z1": {"F": (), "S": (88, 128)},
    "z2": {"F": (), "S": (48,)},
    "after": {
        ("send", "S", 1): (("z2", "F", 0),),
        ("keep", "F"): (("z2", "F", 0),),
        ("moments", "S"): (("core", "F", 0),),
    },
}


def row_keys(order_ref, tile_ref, me, n_bin, per_owner):
    rows = tile_ref.shape[1]
    tiles = n_bin * per_owner
    padded = -(-tiles // 16) * 16
    place = lax.broadcasted_iota(jnp.int32, (padded, rows), 0)
    wanted = jnp.full((padded, rows), -1, jnp.int32)
    for k in range(n_bin):
        for i in range(per_owner):
            wanted = jnp.where(place == k * per_owner + i, order_ref[(me ^ k) * per_owner + i], wanted)
    hits = wanted == tile_ref[...]
    block = 128
    before = lax.broadcasted_iota(jnp.int32, (block, block), 0) < lax.broadcasted_iota(jnp.int32, (block, block), 1)
    before = before.astype(jnp.float32).astype(jnp.bfloat16)
    ones = hits.astype(jnp.float32)
    ranks, seen = [], jnp.zeros((padded, 1), jnp.float32)
    for at in range(0, rows, block):
        here = ones[:, at : at + block]
        ranks.append(seen + jnp.dot(here.astype(jnp.bfloat16), before, preferred_element_type=jnp.float32))
        seen = seen + jnp.sum(here, axis=1, keepdims=True)
    rank = jnp.concatenate(ranks, axis=1)
    return jnp.where(hits, rank, -1.0).astype(jnp.int32)


def placing(keys, instrument, n_bin, per_owner, slots):
    slot = lax.broadcasted_iota(jnp.int32, (slots, keys.shape[1]), 0)
    parts = [
        (slot == keys[k * per_owner + instrument : k * per_owner + instrument + 1, :]).astype(jnp.float32)
        for k in range(n_bin)
    ]
    return jnp.concatenate(parts, axis=0).astype(jnp.bfloat16)


def marked(values, limit, one_at):
    lane = lax.broadcasted_iota(jnp.int32, values.shape, 1)
    ones = jnp.where(lane == one_at, 1.0, 0.0)
    return jnp.where(lane < limit, values.astype(jnp.float32), ones).astype(jnp.bfloat16)


def place_wide(keys, out_refs, part, values, n_bin, per_owner, slots):
    iasi, atms = (placing(keys, instrument, n_bin, per_owner, slots) for instrument in (0, 2))
    placed = jnp.dot(iasi, marked(values, C_IASI, WIDE - 1), preferred_element_type=jnp.float32)
    aside = jnp.dot(atms, marked(values[:, :128], C_ATMS, C_ATMS), preferred_element_type=jnp.float32)
    last = placed[:, WIDE - 128 :] + pltpu.roll(aside, ATMS_AT % 128, 1)
    first, middle, end = part * WIDE, (part + 1) * WIDE - 128, (part + 1) * WIDE
    for k in range(n_bin):
        at = slice(k * slots, (k + 1) * slots)
        out_refs[k][:, first:middle] = placed[at, : WIDE - 128].astype(jnp.bfloat16)
        out_refs[k][:, middle:end] = last[at].astype(jnp.bfloat16)


def place_mid(keys, out_refs, part, values, n_bin, per_owner, slots):
    cris = placing(keys, 1, n_bin, per_owner, slots)
    placed = jnp.dot(cris, marked(values[:, :MID], C_CRIS, CRIS_ONE), preferred_element_type=jnp.float32)
    if part == 1:
        placed = pltpu.roll(placed, CRIS_AN - CRIS_COLUMNS, 1)
    for k in range(n_bin):
        rows = placed[k * slots : (k + 1) * slots]
        if part == 0:
            out_refs[k][:, :MID] = rows.astype(jnp.bfloat16)
        else:
            shared = out_refs[k][:, CRIS_COLUMNS:MID].astype(jnp.float32) + rows[:, : MID - CRIS_COLUMNS]
            out_refs[k][:, CRIS_COLUMNS:MID] = shared.astype(jnp.bfloat16)
            out_refs[k][:, MID:] = rows[:, MID - CRIS_COLUMNS :].astype(jnp.bfloat16)


def first_place_kernel(place, sizes, order_hbm, tile_hbm, bg_hbm, an_hbm, *refs):
    n_bin = sizes[0]
    out_refs, (keys_ref, bg_ref, an_ref, order_ref, tile_ref, sem) = refs[:n_bin], refs[n_bin:]
    copies = [
        pltpu.make_async_copy(source, target, sem.at[i])
        for i, (source, target) in enumerate(
            ((order_hbm, order_ref), (tile_hbm, tile_ref), (bg_hbm, bg_ref), (an_hbm, an_ref))
        )
    ]
    for copy in copies:
        copy.start()
    copies[0].wait()
    copies[1].wait()
    keys = row_keys(order_ref, tile_ref, lax.axis_index("bin"), *sizes[:2])
    keys_ref[...] = keys
    for part, ref in enumerate((bg_ref, an_ref)):
        copies[2 + part].wait()
        place(keys, out_refs, part, ref[...], *sizes)


def second_place_kernel(place, sizes, keys_ref, bg_ref, an_ref, *out_refs):
    for part, ref in enumerate((bg_ref, an_ref)):
        place(keys_ref[...], out_refs, part, ref[...], *sizes)


def offset_of(place, n):
    bits = n.bit_length() - 1
    return sum(1 << i for i in range(bits) if not place >> (bits - 1 - i) & 1)


def moment_kernel(lanes, rows_c, n_cycle, n_in, n_after, *refs):
    in_refs, out_refs, cross_ref = refs[:n_in], refs[n_in + n_after : -1], refs[-1]
    columns, sums_end = (WIDE, WIDE) if lanes == WIDE else (CRIS_COLUMNS, CRIS_ONE + 1)
    whole = in_refs[0].shape[0] // 16 * 16

    def stacked(at):
        ends = [ref[whole:, at : at + lanes].astype(jnp.float32) for ref in in_refs]
        return jnp.concatenate(
            [ref[:whole, at : at + lanes] for ref in in_refs] + [jnp.concatenate(ends).astype(jnp.bfloat16)]
        )

    cross = lax.dot_general(
        stacked(0), stacked(columns), (((0,), (0,)), ((), ())), preferred_element_type=jnp.float32
    )
    cross_ref[:lanes, :] = cross
    if lanes == WIDE:
        lane = lax.broadcasted_iota(jnp.int32, (WIDE - ATMS_AT, 128), 1) + (WIDE - 128)
        cross_ref[: WIDE - ATMS_AT, WIDE - 128 :] = jnp.where(
            (lane >= ATMS_AT) & (lane < WIDE - 1),
            cross_ref[ATMS_AT:, WIDE - 128 :],
            cross_ref[: WIDE - ATMS_AT, WIDE - 128 :],
        )
    else:
        cross_ref[lanes:, :] = jnp.zeros((cross_ref.shape[0] - lanes, lanes), jnp.float32)
    sums = cross_ref[sums_end - SUMS : sums_end, :]
    me = lax.axis_index("cycle")
    segments, end = [], 0
    for place in range(n_cycle):
        segments.append((place, end, end + rows_c))
        end += rows_c
        if place % (n_cycle // 4) == n_cycle // 8 - 1:
            segments.append((None, end, end + SUMS))
            end += SUMS
    start = 0
    for out_ref in out_refs:
        end = start + out_ref.shape[0]
        for place, first, last in segments:
            low, high = max(start, first), min(end, last)
            if low < high:
                if place is None:
                    rows = sums[low - first : high - first]
                else:
                    row = (me ^ offset_of(place, n_cycle)) * rows_c + (low - first)
                    rows = cross_ref[pl.ds(pl.multiple_of(row, 8), high - low), :]
                out_ref[low - start : high - start, :] = rows
        start = end


def covariance(total, one, sums):
    scale = 1.0 / sums[:, one : one + 1]
    return total * scale - (total[:, one : one + 1] * scale) * (sums * scale)


def finish_mid_kernel(rows_c, keep_ref, send_ref, *refs):
    out_ref = refs[-1]
    got = jnp.concatenate([ref[...] for ref in refs[:-1]])
    row = lax.broadcasted_iota(jnp.int32, (rows_c, MID), 0) + lax.axis_index("cycle") * rows_c
    lane = lax.broadcasted_iota(jnp.int32, (rows_c, MID), 1)
    sums = send_ref[send_ref.shape[0] - SUMS :] + got[rows_c:]
    cov = covariance(keep_ref[...] + got[:rows_c], CRIS_AN - CRIS_COLUMNS + CRIS_ONE, sums[SUMS - 1 :])
    cov = pltpu.roll(cov, MID - (CRIS_AN - CRIS_COLUMNS), 1)
    out_ref[:, :MID] = jnp.where((lane < C_CRIS) & (row < C_CRIS), cov, 0.0)
    out_ref[:, MID:] = jnp.zeros((rows_c, WIDE - MID), jnp.float32)


def finish_kernel(rows_c, keep_ref, send_ref, *refs):
    *got_refs, mid_ref, out_ref, wide_ref, atms_ref, sem = refs
    mid_copy = pltpu.make_async_copy(mid_ref, out_ref.at[1], sem.at[1])
    mid_copy.start()
    got = jnp.concatenate([ref[...] for ref in got_refs])
    row = lax.broadcasted_iota(jnp.int32, (rows_c, WIDE), 0) + lax.axis_index("cycle") * rows_c
    lane = lax.broadcasted_iota(jnp.int32, (rows_c, WIDE), 1)
    total = keep_ref[...] + got[:rows_c]
    sums = send_ref[send_ref.shape[0] - SUMS :] + got[rows_c:]
    cov = covariance(total, WIDE - 1, sums[SUMS - 1 :])
    wide_ref[...] = jnp.where((lane < C_IASI) & (row < C_IASI), cov, 0.0)
    wide_copy = pltpu.make_async_copy(wide_ref, out_ref.at[0], sem.at[0])
    wide_copy.start()
    cov = covariance(total[:, WIDE - 128 :], 126, sums[SUMS - 2 : SUMS - 1, WIDE - 128 :])
    cov = pltpu.roll(cov, 128 - ATMS_AT % 128, 1)
    atms_ref[:, :128] = jnp.where((lane[:, :128] < C_ATMS) & (row[:, :128] < C_ATMS), cov, 0.0)
    atms_ref[:, 128:] = jnp.zeros((rows_c, WIDE - 128), jnp.float32)
    atms_copy = pltpu.make_async_copy(atms_ref, out_ref.at[2], sem.at[2])
    atms_copy.start()
    mid_copy.wait()
    wide_copy.wait()
    atms_copy.wait()


def to_owners(parts, order):
    n_bin = len(parts)
    return [parts[0]] + [
        lax.ppermute(parts[k], "bin", [(i, i ^ k) for i in range(n_bin)])
        for k in (order if n_bin == 4 else range(n_bin - 1, 0, -1))
    ]


def swap(value, bit, n):
    return lax.ppermute(value, "cycle", [(i, i ^ bit) for i in range(n)])


def sum_kernel(first, spans, n_after, near_ref, *refs):
    out_ref = refs[-1]
    rows = out_ref.shape[0]
    out_ref[...] = near_ref[first : first + rows]
    for ref, start in zip(refs[: len(spans)], spans):
        low, high = max(first, start), min(first + rows, start + ref.shape[0])
        out_ref[low - first : high - first] += ref[low - start : high - start]


def on_device(obs_minus_bg, obs_minus_an, tile_of_row, owner_order):
    n_bin = lax.axis_size("bin")
    n_cycle = lax.axis_size("cycle")
    rows, width = obs_minus_bg.shape
    tiles = owner_order.shape[0]
    per_owner = tiles // n_bin
    slots = -(-(2 * rows // tiles) // 8) * 8
    rows_c = width // n_cycle
    tile = tile_of_row.reshape(1, rows)
    padded = -(-tiles // 16) * 16
    sizes = (n_bin, per_owner, slots)
    cfg = CFG
    lanes = {"F": MID, "S": WIDE} if cfg["first"] == "M" else {"F": WIDE, "S": MID}
    places = {MID: place_mid, WIDE: place_wide}

    def slot_shapes(p):
        return [jax.ShapeDtypeStruct((slots, 2 * WIDE if lanes[p] == WIDE else CRIS_SLOT), jnp.bfloat16)] * n_bin

    *first, keys, bg, an = pl.pallas_call(
        functools.partial(first_place_kernel, places[lanes["F"]], sizes),
        out_shape=slot_shapes("F")
        + [jax.ShapeDtypeStruct((padded, rows), jnp.int32)]
        + [jax.ShapeDtypeStruct((rows, width), jnp.bfloat16)] * 2,
        in_specs=[HBM] * 4,
        out_specs=[VMEM] * (n_bin + 3),
        scratch_shapes=[
            pltpu.SMEM((tiles,), jnp.int32),
            pltpu.VMEM((1, rows), jnp.int32),
            pltpu.SemaphoreType.DMA((4,)),
        ],
        compiler_params=PARAMS,
    )(*(pltpu.with_memory_space_constraint(x, pltpu.HBM) for x in (owner_order, tile, obs_minus_bg, obs_minus_an)))
    second = pl.pallas_call(
        functools.partial(second_place_kernel, places[lanes["S"]], sizes),
        out_shape=slot_shapes("S"),
        in_specs=[VMEM] * 3,
        out_specs=[VMEM] * n_bin,
        compiler_params=PARAMS,
    )(keys, bg, an)
    owned = {"F": to_owners(first, cfg["order"]["F"]), "S": to_owners(second, cfg["order"]["S"])}

    kept = n_cycle // 8 * rows_c
    sent = kept + SUMS
    half = 2 * (sent + kept)

    def bounds(cuts, end):
        return list(zip([0, *cuts], [*cuts, end]))

    core_spans = {p: bounds(cfg["core"][p], half) for p in "FS"}
    z1_spans = {p: bounds(cfg["z1"][p], sent + kept) for p in "FS"}
    z2_spans = {p: bounds(cfg["z2"][p], sent) for p in "FS"}
    memo, busy = {}, set()

    def get(name):
        if name not in memo:
            assert name not in busy
            busy.add(name)
            memo[name] = make(*name)
            busy.discard(name)
        return memo[name]

    def after(*name):
        return [get(n) for n in cfg["after"].get(name, ())]

    def overlapping(kind, p, spans, low, high, shift=0):
        hits = [(i, start + shift) for i, (start, end) in enumerate(spans) if start + shift < high and low < end + shift]
        return [get((kind, p, i)) for i, _ in hits], [start for _, start in hits]

    def summed(p, low, high, z1, waits):
        terms, starts = overlapping("core", p, core_spans[p], low, high)
        if z1:
            more, more_starts = overlapping("z1", p, z1_spans[p], low, high, sent + kept)
            terms, starts = terms + more, starts + more_starts
        return pl.pallas_call(
            functools.partial(sum_kernel, low, starts, len(waits)),
            out_shape=jax.ShapeDtypeStruct((high - low, lanes[p]), jnp.float32),
            in_specs=[VMEM] * (1 + len(terms)) + [ANY] * len(waits),
            out_specs=VMEM,
            compiler_params=PARAMS,
        )(get(("moments", p))[-1], *terms, *waits)

    def make(kind, p, i=None):
        if kind == "moments":
            waits = after(kind, p)
            shapes = [end - start for start, end in core_spans[p]] + [half]
            return pl.pallas_call(
                functools.partial(moment_kernel, lanes[p], rows_c, n_cycle, n_bin, len(waits)),
                out_shape=[jax.ShapeDtypeStruct((size, lanes[p]), jnp.float32) for size in shapes],
                in_specs=[VMEM] * n_bin + [ANY] * len(waits),
                out_specs=[VMEM] * len(shapes),
                scratch_shapes=[pltpu.VMEM((WIDE, lanes[p]), jnp.float32)],
                compiler_params=PARAMS,
            )(*owned[p], *waits)
        if kind == "got":
            return owned[p][i]
        if kind == "core":
            return swap(get(("moments", p))[i], 1, n_cycle)
        if kind == "z1":
            low, high = z1_spans[p][i]
            return swap(summed(p, low, high, False, after(kind, p, i)), 2, n_cycle)
        if kind == "send":
            low, high = z2_spans[p][i]
            return summed(p, low + sent + kept, high + sent + kept, True, after(kind, p, i))
        if kind == "z2":
            return swap(get(("send", p, i)), 4, n_cycle)
        if kind == "keep":
            return summed(p, half - kept, half, True, after(kind, p))

    def ends(p):
        n = len(z2_spans[p])
        keep, send, got = get(("keep", p)), get(("send", p, n - 1)), [get(("z2", p, i)) for i in range(n)]
        bit = 8
        while bit < n_cycle:
            got = jnp.concatenate(got)
            part = keep.shape[0] // 2
            send = jnp.concatenate([keep[:part] + got[:part], send[-SUMS:] + got[-SUMS:]])
            keep, got = keep[part:] + got[part:-SUMS], [swap(send, bit, n_cycle)]
            bit *= 2
        return [keep, send, *got]

    wide, mid = (ends(p) for p in sorted("FS", key=lambda p: -lanes[p]))
    mid = pl.pallas_call(
        functools.partial(finish_mid_kernel, rows_c),
        out_shape=jax.ShapeDtypeStruct((rows_c, width), jnp.float32),
        in_specs=[VMEM] * len(mid),
        out_specs=VMEM,
        compiler_params=PARAMS,
    )(*mid)
    return pl.pallas_call(
        functools.partial(finish_kernel, rows_c),
        out_shape=jax.ShapeDtypeStruct((per_owner, rows_c, width), jnp.float32),
        in_specs=[VMEM] * (len(wide) + 1),
        out_specs=HBM,
        scratch_shapes=[
            pltpu.VMEM((rows_c, width), jnp.float32),
            pltpu.VMEM((rows_c, width), jnp.float32),
            pltpu.SemaphoreType.DMA((3,)),
        ],
        compiler_params=PARAMS,
    )(*wide, mid)


def solution(mesh):
    return jax.shard_map(
        on_device,
        mesh=mesh,
        in_specs=(
            P(("cycle", "bin"), None),
            P(("cycle", "bin"), None),
            P(("cycle", "bin"), None),
            P(),
        ),
        out_specs=P("bin", "cycle", None),
        check_vma=False,
    )
```

```python
import functools

import jax
import jax.numpy as jnp
from jax import lax
from jax.experimental import pallas as pl
from jax.experimental.pallas import tpu as pltpu
from jax.sharding import PartitionSpec as P

C_IASI = 616
C_CRIS = 431
C_ATMS = 22
WIDE = 640
ATMS_AT = 616
MID = 512
CRIS_ONE = 431
CRIS_AN = 432
CRIS_COLUMNS = 384
CRIS_SLOT = CRIS_COLUMNS + MID
SUMS = 8

VMEM = pl.BlockSpec(memory_space=pltpu.VMEM)
HBM = pl.BlockSpec(memory_space=pltpu.HBM)
ANY = pl.BlockSpec(memory_space=pl.ANY)
PARAMS = pltpu.CompilerParams(vmem_limit_bytes=48 * 1024 * 1024)


CFG = {
    "first": "M",
    "order": {"F": (3, 2, 1), "S": (2, 1, 3)},
    "core": {"F": (88, 168), "S": (40, 136, 144, 168, 256)},
    "z1": {"F": (), "S": (88, 128)},
    "z2": {"F": (), "S": (48,)},
    "after": {
        ("send", "S", 1): (("z2", "F", 0),),
        ("keep", "F"): (("z2", "F", 0),),
        ("moments", "S"): (("core", "F", 0),),
    },
}


def row_keys(order_ref, tile_ref, me, n_bin, per_owner):
    rows = tile_ref.shape[1]
    tiles = n_bin * per_owner
    padded = -(-tiles // 16) * 16
    place = lax.broadcasted_iota(jnp.int32, (padded, rows), 0)
    wanted = jnp.full((padded, rows), -1, jnp.int32)
    for k in range(n_bin):
        for i in range(per_owner):
            wanted = jnp.where(place == k * per_owner + i, order_ref[(me ^ k) * per_owner + i], wanted)
    hits = wanted == tile_ref[...]
    block = 128
    before = lax.broadcasted_iota(jnp.int32, (block, block), 0) < lax.broadcasted_iota(jnp.int32, (block, block), 1)
    before = before.astype(jnp.float32).astype(jnp.bfloat16)
    ones = hits.astype(jnp.float32)
    ranks, seen = [], jnp.zeros((padded, 1), jnp.float32)
    for at in range(0, rows, block):
        here = ones[:, at : at + block]
        ranks.append(seen + jnp.dot(here.astype(jnp.bfloat16), before, preferred_element_type=jnp.float32))
        seen = seen + jnp.sum(here, axis=1, keepdims=True)
    rank = jnp.concatenate(ranks, axis=1)
    return jnp.where(hits, rank, -1.0).astype(jnp.int32)


def placing(keys, instrument, n_bin, per_owner, slots):
    slot = lax.broadcasted_iota(jnp.int32, (slots, keys.shape[1]), 0)
    parts = [
        (slot == keys[k * per_owner + instrument : k * per_owner + instrument + 1, :]).astype(jnp.float32)
        for k in range(n_bin)
    ]
    return jnp.concatenate(parts, axis=0).astype(jnp.bfloat16)


def marked(values, limit, one_at):
    first = limit // 128 * 128
    last = values[:, first : first + 128]
    lane = lax.broadcasted_iota(jnp.int32, last.shape, 1) + first
    last = jnp.where(lane < limit, last.astype(jnp.float32), jnp.where(lane == one_at, 1.0, 0.0)).astype(jnp.bfloat16)
    return jnp.concatenate([values[:, :first], last], axis=1) if first else last


def place_wide(keys, out_refs, part, values, n_bin, per_owner, slots):
    iasi, atms = (placing(keys, instrument, n_bin, per_owner, slots) for instrument in (0, 2))
    placed = jnp.dot(iasi, marked(values, C_IASI, WIDE - 1), preferred_element_type=jnp.float32)
    aside = jnp.dot(atms, marked(values[:, :128], C_ATMS, C_ATMS), preferred_element_type=jnp.float32)
    last = placed[:, WIDE - 128 :] + pltpu.roll(aside, ATMS_AT % 128, 1)
    first, middle, end = part * WIDE, (part + 1) * WIDE - 128, (part + 1) * WIDE
    for k in range(n_bin):
        at = slice(k * slots, (k + 1) * slots)
        out_refs[k][:, first:middle] = placed[at, : WIDE - 128].astype(jnp.bfloat16)
        out_refs[k][:, middle:end] = last[at].astype(jnp.bfloat16)


def place_mid(keys, out_refs, part, values, n_bin, per_owner, slots):
    cris = placing(keys, 1, n_bin, per_owner, slots)
    placed = jnp.dot(cris, marked(values[:, :MID], C_CRIS, CRIS_ONE), preferred_element_type=jnp.float32)
    if part == 1:
        placed = pltpu.roll(placed, CRIS_AN - CRIS_COLUMNS, 1)
    for k in range(n_bin):
        rows = placed[k * slots : (k + 1) * slots]
        if part == 0:
            out_refs[k][:, :MID] = rows.astype(jnp.bfloat16)
        else:
            shared = out_refs[k][:, CRIS_COLUMNS:MID].astype(jnp.float32) + rows[:, : MID - CRIS_COLUMNS]
            out_refs[k][:, CRIS_COLUMNS:MID] = shared.astype(jnp.bfloat16)
            out_refs[k][:, MID:] = rows[:, MID - CRIS_COLUMNS :].astype(jnp.bfloat16)


def first_place_kernel(place, sizes, order_hbm, tile_hbm, bg_hbm, an_hbm, *refs):
    n_bin = sizes[0]
    out_refs, (keys_ref, bg_ref, an_ref, order_ref, tile_ref, sem) = refs[:n_bin], refs[n_bin:]
    copies = [
        pltpu.make_async_copy(source, target, sem.at[i])
        for i, (source, target) in enumerate(
            ((order_hbm, order_ref), (tile_hbm, tile_ref), (bg_hbm, bg_ref), (an_hbm, an_ref))
        )
    ]
    for copy in copies:
        copy.start()
    copies[0].wait()
    copies[1].wait()
    keys = row_keys(order_ref, tile_ref, lax.axis_index("bin"), *sizes[:2])
    keys_ref[...] = keys
    for part, ref in enumerate((bg_ref, an_ref)):
        copies[2 + part].wait()
        place(keys, out_refs, part, ref[...], *sizes)


def second_place_kernel(place, sizes, keys_ref, bg_ref, an_ref, *out_refs):
    for part, ref in enumerate((bg_ref, an_ref)):
        place(keys_ref[...], out_refs, part, ref[...], *sizes)


def offset_of(place, n):
    bits = n.bit_length() - 1
    return sum(1 << i for i in range(bits) if not place >> (bits - 1 - i) & 1)


def moment_kernel(lanes, rows_c, n_cycle, n_in, n_after, *refs):
    in_refs, out_refs, cross_ref = refs[:n_in], refs[n_in + n_after : -1], refs[-1]
    columns, sums_end = (WIDE, WIDE) if lanes == WIDE else (CRIS_COLUMNS, CRIS_ONE + 1)
    whole = in_refs[0].shape[0] // 16 * 16

    def stacked(at):
        ends = [ref[whole:, at : at + lanes].astype(jnp.float32) for ref in in_refs]
        return jnp.concatenate(
            [ref[:whole, at : at + lanes] for ref in in_refs] + [jnp.concatenate(ends).astype(jnp.bfloat16)]
        )

    cross = lax.dot_general(
        stacked(0), stacked(columns), (((0,), (0,)), ((), ())), preferred_element_type=jnp.float32
    )
    cross_ref[:lanes, :] = cross
    if lanes == WIDE:
        lane = lax.broadcasted_iota(jnp.int32, (WIDE - ATMS_AT, 128), 1) + (WIDE - 128)
        cross_ref[: WIDE - ATMS_AT, WIDE - 128 :] = jnp.where(
            (lane >= ATMS_AT) & (lane < WIDE - 1),
            cross_ref[ATMS_AT:, WIDE - 128 :],
            cross_ref[: WIDE - ATMS_AT, WIDE - 128 :],
        )
    else:
        cross_ref[lanes:, :] = jnp.zeros((cross_ref.shape[0] - lanes, lanes), jnp.float32)
    sums = cross_ref[sums_end - SUMS : sums_end, :]
    me = lax.axis_index("cycle")
    segments, end = [], 0
    for place in range(n_cycle):
        segments.append((place, end, end + rows_c))
        end += rows_c
        if place % (n_cycle // 4) == n_cycle // 8 - 1:
            segments.append((None, end, end + SUMS))
            end += SUMS
    start = 0
    for out_ref in out_refs:
        end = start + out_ref.shape[0]
        for place, first, last in segments:
            low, high = max(start, first), min(end, last)
            if low < high:
                if place is None:
                    rows = sums[low - first : high - first]
                else:
                    row = (me ^ offset_of(place, n_cycle)) * rows_c + (low - first)
                    rows = cross_ref[pl.ds(pl.multiple_of(row, 8), high - low), :]
                out_ref[low - start : high - start, :] = rows
        start = end


def covariance(total, one, sums):
    scale = 1.0 / sums[:, one : one + 1]
    return total * scale - (total[:, one : one + 1] * scale) * (sums * scale)


def finish_mid_kernel(rows_c, keep_ref, send_ref, *refs):
    out_ref = refs[-1]
    got = jnp.concatenate([ref[...] for ref in refs[:-1]])
    row = lax.broadcasted_iota(jnp.int32, (rows_c, MID), 0) + lax.axis_index("cycle") * rows_c
    lane = lax.broadcasted_iota(jnp.int32, (rows_c, MID), 1)
    sums = send_ref[send_ref.shape[0] - SUMS :] + got[rows_c:]
    cov = covariance(keep_ref[...] + got[:rows_c], CRIS_AN - CRIS_COLUMNS + CRIS_ONE, sums[SUMS - 1 :])
    cov = pltpu.roll(cov, MID - (CRIS_AN - CRIS_COLUMNS), 1)
    out_ref[:, :MID] = jnp.where((lane < C_CRIS) & (row < C_CRIS), cov, 0.0)
    out_ref[:, MID:] = jnp.zeros((rows_c, WIDE - MID), jnp.float32)


def finish_kernel(rows_c, keep_ref, send_ref, *refs):
    *got_refs, mid_ref, out_ref, wide_ref, atms_ref, sem = refs
    mid_copy = pltpu.make_async_copy(mid_ref, out_ref.at[1], sem.at[1])
    mid_copy.start()
    got = jnp.concatenate([ref[...] for ref in got_refs])
    row = lax.broadcasted_iota(jnp.int32, (rows_c, WIDE), 0) + lax.axis_index("cycle") * rows_c
    lane = lax.broadcasted_iota(jnp.int32, (rows_c, WIDE), 1)
    total = keep_ref[...] + got[:rows_c]
    sums = send_ref[send_ref.shape[0] - SUMS :] + got[rows_c:]
    cov = covariance(total, WIDE - 1, sums[SUMS - 1 :])
    wide_ref[...] = jnp.where((lane < C_IASI) & (row < C_IASI), cov, 0.0)
    wide_copy = pltpu.make_async_copy(wide_ref, out_ref.at[0], sem.at[0])
    wide_copy.start()
    cov = covariance(total[:, WIDE - 128 :], 126, sums[SUMS - 2 : SUMS - 1, WIDE - 128 :])
    cov = pltpu.roll(cov, 128 - ATMS_AT % 128, 1)
    atms_ref[:, :128] = jnp.where((lane[:, :128] < C_ATMS) & (row[:, :128] < C_ATMS), cov, 0.0)
    atms_ref[:, 128:] = jnp.zeros((rows_c, WIDE - 128), jnp.float32)
    atms_copy = pltpu.make_async_copy(atms_ref, out_ref.at[2], sem.at[2])
    atms_copy.start()
    mid_copy.wait()
    wide_copy.wait()
    atms_copy.wait()


def to_owners(parts, order):
    n_bin = len(parts)
    return [parts[0]] + [
        lax.ppermute(parts[k], "bin", [(i, i ^ k) for i in range(n_bin)])
        for k in (order if n_bin == 4 else range(n_bin - 1, 0, -1))
    ]


def swap(value, bit, n):
    return lax.ppermute(value, "cycle", [(i, i ^ bit) for i in range(n)])


def sum_kernel(first, spans, n_after, near_ref, *refs):
    out_ref = refs[-1]
    rows = out_ref.shape[0]
    out_ref[...] = near_ref[first : first + rows]
    for ref, start in zip(refs[: len(spans)], spans):
        low, high = max(first, start), min(first + rows, start + ref.shape[0])
        out_ref[low - first : high - first] += ref[low - start : high - start]


def on_device(obs_minus_bg, obs_minus_an, tile_of_row, owner_order):
    n_bin = lax.axis_size("bin")
    n_cycle = lax.axis_size("cycle")
    rows, width = obs_minus_bg.shape
    tiles = owner_order.shape[0]
    per_owner = tiles // n_bin
    slots = -(-(2 * rows // tiles) // 8) * 8
    rows_c = width // n_cycle
    tile = tile_of_row.reshape(1, rows)
    padded = -(-tiles // 16) * 16
    sizes = (n_bin, per_owner, slots)
    cfg = CFG
    lanes = {"F": MID, "S": WIDE} if cfg["first"] == "M" else {"F": WIDE, "S": MID}
    places = {MID: place_mid, WIDE: place_wide}

    def slot_shapes(p):
        return [jax.ShapeDtypeStruct((slots, 2 * WIDE if lanes[p] == WIDE else CRIS_SLOT), jnp.bfloat16)] * n_bin

    *first, keys, bg, an = pl.pallas_call(
        functools.partial(first_place_kernel, places[lanes["F"]], sizes),
        out_shape=slot_shapes("F")
        + [jax.ShapeDtypeStruct((padded, rows), jnp.int32)]
        + [jax.ShapeDtypeStruct((rows, width), jnp.bfloat16)] * 2,
        in_specs=[HBM] * 4,
        out_specs=[VMEM] * (n_bin + 3),
        scratch_shapes=[
            pltpu.SMEM((tiles,), jnp.int32),
            pltpu.VMEM((1, rows), jnp.int32),
            pltpu.SemaphoreType.DMA((4,)),
        ],
        compiler_params=PARAMS,
    )(*(pltpu.with_memory_space_constraint(x, pltpu.HBM) for x in (owner_order, tile, obs_minus_bg, obs_minus_an)))
    second = pl.pallas_call(
        functools.partial(second_place_kernel, places[lanes["S"]], sizes),
        out_shape=slot_shapes("S"),
        in_specs=[VMEM] * 3,
        out_specs=[VMEM] * n_bin,
        compiler_params=PARAMS,
    )(keys, bg, an)
    owned = {"F": to_owners(first, cfg["order"]["F"]), "S": to_owners(second, cfg["order"]["S"])}

    kept = n_cycle // 8 * rows_c
    sent = kept + SUMS
    half = 2 * (sent + kept)

    def bounds(cuts, end):
        return list(zip([0, *cuts], [*cuts, end]))

    core_spans = {p: bounds(cfg["core"][p], half) for p in "FS"}
    z1_spans = {p: bounds(cfg["z1"][p], sent + kept) for p in "FS"}
    z2_spans = {p: bounds(cfg["z2"][p], sent) for p in "FS"}
    memo, busy = {}, set()

    def get(name):
        if name not in memo:
            assert name not in busy
            busy.add(name)
            memo[name] = make(*name)
            busy.discard(name)
        return memo[name]

    def after(*name):
        return [get(n) for n in cfg["after"].get(name, ())]

    def overlapping(kind, p, spans, low, high, shift=0):
        hits = [(i, start + shift) for i, (start, end) in enumerate(spans) if start + shift < high and low < end + shift]
        return [get((kind, p, i)) for i, _ in hits], [start for _, start in hits]

    def summed(p, low, high, z1, waits):
        terms, starts = overlapping("core", p, core_spans[p], low, high)
        if z1:
            more, more_starts = overlapping("z1", p, z1_spans[p], low, high, sent + kept)
            terms, starts = terms + more, starts + more_starts
        return pl.pallas_call(
            functools.partial(sum_kernel, low, starts, len(waits)),
            out_shape=jax.ShapeDtypeStruct((high - low, lanes[p]), jnp.float32),
            in_specs=[VMEM] * (1 + len(terms)) + [ANY] * len(waits),
            out_specs=VMEM,
            compiler_params=PARAMS,
        )(get(("moments", p))[-1], *terms, *waits)

    def make(kind, p, i=None):
        if kind == "moments":
            waits = after(kind, p)
            shapes = [end - start for start, end in core_spans[p]] + [half]
            return pl.pallas_call(
                functools.partial(moment_kernel, lanes[p], rows_c, n_cycle, n_bin, len(waits)),
                out_shape=[jax.ShapeDtypeStruct((size, lanes[p]), jnp.float32) for size in shapes],
                in_specs=[VMEM] * n_bin + [ANY] * len(waits),
                out_specs=[VMEM] * len(shapes),
                scratch_shapes=[pltpu.VMEM((WIDE, lanes[p]), jnp.float32)],
                compiler_params=PARAMS,
            )(*owned[p], *waits)
        if kind == "got":
            return owned[p][i]
        if kind == "core":
            return swap(get(("moments", p))[i], 1, n_cycle)
        if kind == "z1":
            low, high = z1_spans[p][i]
            return swap(summed(p, low, high, False, after(kind, p, i)), 2, n_cycle)
        if kind == "send":
            low, high = z2_spans[p][i]
            return summed(p, low + sent + kept, high + sent + kept, True, after(kind, p, i))
        if kind == "z2":
            return swap(get(("send", p, i)), 4, n_cycle)
        if kind == "keep":
            return summed(p, half - kept, half, True, after(kind, p))

    def ends(p):
        n = len(z2_spans[p])
        keep, send, got = get(("keep", p)), get(("send", p, n - 1)), [get(("z2", p, i)) for i in range(n)]
        bit = 8
        while bit < n_cycle:
            got = jnp.concatenate(got)
            part = keep.shape[0] // 2
            send = jnp.concatenate([keep[:part] + got[:part], send[-SUMS:] + got[-SUMS:]])
            keep, got = keep[part:] + got[part:-SUMS], [swap(send, bit, n_cycle)]
            bit *= 2
        return [keep, send, *got]

    wide, mid = (ends(p) for p in sorted("FS", key=lambda p: -lanes[p]))
    mid = pl.pallas_call(
        functools.partial(finish_mid_kernel, rows_c),
        out_shape=jax.ShapeDtypeStruct((rows_c, width), jnp.float32),
        in_specs=[VMEM] * len(mid),
        out_specs=VMEM,
        compiler_params=PARAMS,
    )(*mid)
    return pl.pallas_call(
        functools.partial(finish_kernel, rows_c),
        out_shape=jax.ShapeDtypeStruct((per_owner, rows_c, width), jnp.float32),
        in_specs=[VMEM] * (len(wide) + 1),
        out_specs=HBM,
        scratch_shapes=[
            pltpu.VMEM((rows_c, width), jnp.float32),
            pltpu.VMEM((rows_c, width), jnp.float32),
            pltpu.SemaphoreType.DMA((3,)),
        ],
        compiler_params=PARAMS,
    )(*wide, mid)


def solution(mesh):
    return jax.shard_map(
        on_device,
        mesh=mesh,
        in_specs=(
            P(("cycle", "bin"), None),
            P(("cycle", "bin"), None),
            P(("cycle", "bin"), None),
            P(),
        ),
        out_specs=P("bin", "cycle", None),
        check_vma=False,
    )
```

```python
import functools

import jax
import jax.numpy as jnp
from jax import lax
from jax.experimental import pallas as pl
from jax.experimental.pallas import tpu as pltpu
from jax.sharding import PartitionSpec as P

C_IASI = 616
C_CRIS = 431
C_ATMS = 22
WIDE = 640
ATMS_AT = 616
MID = 512
CRIS_ONE = 431
CRIS_AN = 432
CRIS_COLUMNS = 384
CRIS_SLOT = CRIS_COLUMNS + MID
SUMS = 8

VMEM = pl.BlockSpec(memory_space=pltpu.VMEM)
HBM = pl.BlockSpec(memory_space=pltpu.HBM)
ANY = pl.BlockSpec(memory_space=pl.ANY)
PARAMS = pltpu.CompilerParams(vmem_limit_bytes=48 * 1024 * 1024)


CFG = {
    "first": "M",
    "order": {"F": (3, 2, 1), "S": (2, 1, 3)},
    "core": {"F": (88, 168), "S": (40, 136, 144, 168, 256)},
    "z1": {"F": (), "S": (88, 128)},
    "z2": {"F": (), "S": (48,)},
    "after": {
        ("send", "S", 1): (("z2", "F", 0),),
        ("keep", "F"): (("z2", "F", 0),),
        ("moments", "S"): (("core", "F", 0),),
    },
}


def row_keys(order_ref, tile_ref, me, n_bin, per_owner):
    rows = tile_ref.shape[1]
    tiles = n_bin * per_owner
    padded = -(-tiles // 16) * 16
    place = lax.broadcasted_iota(jnp.int32, (padded, rows), 0)
    wanted = jnp.full((padded, rows), -1, jnp.int32)
    for k in range(n_bin):
        for i in range(per_owner):
            wanted = jnp.where(place == k * per_owner + i, order_ref[(me ^ k) * per_owner + i], wanted)
    hits = wanted == tile_ref[...]
    block = 128
    before = lax.broadcasted_iota(jnp.int32, (block, block), 0) < lax.broadcasted_iota(jnp.int32, (block, block), 1)
    before = before.astype(jnp.float32).astype(jnp.bfloat16)
    ones = hits.astype(jnp.float32)
    ranks, seen = [], jnp.zeros((padded, 1), jnp.float32)
    for at in range(0, rows, block):
        here = ones[:, at : at + block]
        ranks.append(seen + jnp.dot(here.astype(jnp.bfloat16), before, preferred_element_type=jnp.float32))
        seen = seen + jnp.sum(here, axis=1, keepdims=True)
    rank = jnp.concatenate(ranks, axis=1)
    return jnp.where(hits, rank, -1.0).astype(jnp.int32)


def placing(keys, instrument, n_bin, per_owner, slots):
    slot = lax.broadcasted_iota(jnp.int32, (slots, keys.shape[1]), 0)
    parts = [
        (slot == keys[k * per_owner + instrument : k * per_owner + instrument + 1, :]).astype(jnp.float32)
        for k in range(n_bin)
    ]
    return jnp.concatenate(parts, axis=0).astype(jnp.bfloat16)


def marked(values, limit, one_at):
    first = limit // 128 * 128
    last = values[:, first : first + 128]
    lane = lax.broadcasted_iota(jnp.int32, last.shape, 1) + first
    last = jnp.where(lane < limit, last.astype(jnp.float32), jnp.where(lane == one_at, 1.0, 0.0)).astype(jnp.bfloat16)
    return jnp.concatenate([values[:, :first], last], axis=1) if first else last


def place_wide(keys, out_refs, part, values, n_bin, per_owner, slots):
    iasi, atms = (placing(keys, instrument, n_bin, per_owner, slots) for instrument in (0, 2))
    placed = jnp.dot(iasi, marked(values, C_IASI, WIDE - 1), preferred_element_type=jnp.float32)
    aside = jnp.dot(atms, marked(values[:, :128], C_ATMS, C_ATMS), preferred_element_type=jnp.float32)
    last = placed[:, WIDE - 128 :] + pltpu.roll(aside, ATMS_AT % 128, 1)
    first, middle, end = part * WIDE, (part + 1) * WIDE - 128, (part + 1) * WIDE
    for k in range(n_bin):
        at = slice(k * slots, (k + 1) * slots)
        out_refs[k][:, first:middle] = placed[at, : WIDE - 128].astype(jnp.bfloat16)
        out_refs[k][:, middle:end] = last[at].astype(jnp.bfloat16)


def place_mid(keys, out_refs, part, values, n_bin, per_owner, slots):
    cris = placing(keys, 1, n_bin, per_owner, slots)
    placed = jnp.dot(cris, marked(values[:, :MID], C_CRIS, CRIS_ONE), preferred_element_type=jnp.float32)
    if part == 1:
        placed = pltpu.roll(placed, CRIS_AN - CRIS_COLUMNS, 1)
    for k in range(n_bin):
        rows = placed[k * slots : (k + 1) * slots]
        if part == 0:
            out_refs[k][:, :MID] = rows.astype(jnp.bfloat16)
        else:
            shared = out_refs[k][:, CRIS_COLUMNS:MID].astype(jnp.float32) + rows[:, : MID - CRIS_COLUMNS]
            out_refs[k][:, CRIS_COLUMNS:MID] = shared.astype(jnp.bfloat16)
            out_refs[k][:, MID:] = rows[:, MID - CRIS_COLUMNS :].astype(jnp.bfloat16)


def first_place_kernel(place, sizes, order_hbm, tile_hbm, bg_hbm, an_hbm, *refs):
    n_bin = sizes[0]
    out_refs, (keys_ref, bg_ref, an_ref, order_ref, tile_ref, sem) = refs[:n_bin], refs[n_bin:]
    pairs = [(order_hbm, order_ref), (tile_hbm, tile_ref)]
    for low, high in ((0, MID), (MID, WIDE)):
        lanes = pl.ds(low, high - low)
        pairs += [(bg_hbm.at[:, lanes], bg_ref.at[:, lanes]), (an_hbm.at[:, lanes], an_ref.at[:, lanes])]
    copies = [pltpu.make_async_copy(*pair, sem.at[i]) for i, pair in enumerate(pairs)]
    for copy in copies:
        copy.start()
    copies[0].wait()
    copies[1].wait()
    keys = row_keys(order_ref, tile_ref, lax.axis_index("bin"), *sizes[:2])
    keys_ref[...] = keys
    for part, ref in enumerate((bg_ref, an_ref)):
        copies[2 + part].wait()
        place(keys, out_refs, part, ref[:, :MID], *sizes)
    copies[4].wait()
    copies[5].wait()


def second_place_kernel(place, sizes, keys_ref, bg_ref, an_ref, *out_refs):
    for part, ref in enumerate((bg_ref, an_ref)):
        place(keys_ref[...], out_refs, part, ref[...], *sizes)


def offset_of(place, n):
    bits = n.bit_length() - 1
    return sum(1 << i for i in range(bits) if not place >> (bits - 1 - i) & 1)


def moment_kernel(lanes, rows_c, n_cycle, n_in, n_after, *refs):
    in_refs, out_refs, cross_ref = refs[:n_in], refs[n_in + n_after : -1], refs[-1]
    columns, sums_end = (WIDE, WIDE) if lanes == WIDE else (CRIS_COLUMNS, CRIS_ONE + 1)
    whole = in_refs[0].shape[0] // 16 * 16

    def stacked(at):
        ends = [ref[whole:, at : at + lanes].astype(jnp.float32) for ref in in_refs]
        return jnp.concatenate(
            [ref[:whole, at : at + lanes] for ref in in_refs] + [jnp.concatenate(ends).astype(jnp.bfloat16)]
        )

    cross = lax.dot_general(
        stacked(0), stacked(columns), (((0,), (0,)), ((), ())), preferred_element_type=jnp.float32
    )
    cross_ref[:lanes, :] = cross
    if lanes == WIDE:
        lane = lax.broadcasted_iota(jnp.int32, (WIDE - ATMS_AT, 128), 1) + (WIDE - 128)
        cross_ref[: WIDE - ATMS_AT, WIDE - 128 :] = jnp.where(
            (lane >= ATMS_AT) & (lane < WIDE - 1),
            cross_ref[ATMS_AT:, WIDE - 128 :],
            cross_ref[: WIDE - ATMS_AT, WIDE - 128 :],
        )
    else:
        cross_ref[lanes:, :] = jnp.zeros((cross_ref.shape[0] - lanes, lanes), jnp.float32)
    sums = cross_ref[sums_end - SUMS : sums_end, :]
    me = lax.axis_index("cycle")
    segments, end = [], 0
    for place in range(n_cycle):
        segments.append((place, end, end + rows_c))
        end += rows_c
        if place % (n_cycle // 4) == n_cycle // 8 - 1:
            segments.append((None, end, end + SUMS))
            end += SUMS
    start = 0
    for out_ref in out_refs:
        end = start + out_ref.shape[0]
        for place, first, last in segments:
            low, high = max(start, first), min(end, last)
            if low < high:
                if place is None:
                    rows = sums[low - first : high - first]
                else:
                    row = (me ^ offset_of(place, n_cycle)) * rows_c + (low - first)
                    rows = cross_ref[pl.ds(pl.multiple_of(row, 8), high - low), :]
                out_ref[low - start : high - start, :] = rows
        start = end


def covariance(total, one, sums):
    scale = 1.0 / sums[:, one : one + 1]
    return total * scale - (total[:, one : one + 1] * scale) * (sums * scale)


def finish_mid_kernel(rows_c, keep_ref, send_ref, *refs):
    out_ref = refs[-1]
    got = jnp.concatenate([ref[...] for ref in refs[:-1]])
    row = lax.broadcasted_iota(jnp.int32, (rows_c, MID), 0) + lax.axis_index("cycle") * rows_c
    lane = lax.broadcasted_iota(jnp.int32, (rows_c, MID), 1)
    sums = send_ref[send_ref.shape[0] - SUMS :] + got[rows_c:]
    cov = covariance(keep_ref[...] + got[:rows_c], CRIS_AN - CRIS_COLUMNS + CRIS_ONE, sums[SUMS - 1 :])
    cov = pltpu.roll(cov, MID - (CRIS_AN - CRIS_COLUMNS), 1)
    out_ref[:, :MID] = jnp.where((lane < C_CRIS) & (row < C_CRIS), cov, 0.0)
    out_ref[:, MID:] = jnp.zeros((rows_c, WIDE - MID), jnp.float32)


def finish_kernel(rows_c, keep_ref, send_ref, *refs):
    *got_refs, mid_ref, out_ref, wide_ref, atms_ref, sem = refs
    mid_copy = pltpu.make_async_copy(mid_ref, out_ref.at[1], sem.at[1])
    mid_copy.start()
    got = jnp.concatenate([ref[...] for ref in got_refs])
    row = lax.broadcasted_iota(jnp.int32, (rows_c, WIDE), 0) + lax.axis_index("cycle") * rows_c
    lane = lax.broadcasted_iota(jnp.int32, (rows_c, WIDE), 1)
    total = keep_ref[...] + got[:rows_c]
    sums = send_ref[send_ref.shape[0] - SUMS :] + got[rows_c:]
    cov = covariance(total, WIDE - 1, sums[SUMS - 1 :])
    wide_ref[...] = jnp.where((lane < C_IASI) & (row < C_IASI), cov, 0.0)
    wide_copy = pltpu.make_async_copy(wide_ref, out_ref.at[0], sem.at[0])
    wide_copy.start()
    cov = covariance(total[:, WIDE - 128 :], 126, sums[SUMS - 2 : SUMS - 1, WIDE - 128 :])
    cov = pltpu.roll(cov, 128 - ATMS_AT % 128, 1)
    atms_ref[:, :128] = jnp.where((lane[:, :128] < C_ATMS) & (row[:, :128] < C_ATMS), cov, 0.0)
    atms_ref[:, 128:] = jnp.zeros((rows_c, WIDE - 128), jnp.float32)
    atms_copy = pltpu.make_async_copy(atms_ref, out_ref.at[2], sem.at[2])
    atms_copy.start()
    mid_copy.wait()
    wide_copy.wait()
    atms_copy.wait()


def to_owners(parts, order):
    n_bin = len(parts)
    return [parts[0]] + [
        lax.ppermute(parts[k], "bin", [(i, i ^ k) for i in range(n_bin)])
        for k in (order if n_bin == 4 else range(n_bin - 1, 0, -1))
    ]


def swap(value, bit, n):
    return lax.ppermute(value, "cycle", [(i, i ^ bit) for i in range(n)])


def sum_kernel(first, spans, n_after, near_ref, *refs):
    out_ref = refs[-1]
    rows = out_ref.shape[0]
    out_ref[...] = near_ref[first : first + rows]
    for ref, start in zip(refs[: len(spans)], spans):
        low, high = max(first, start), min(first + rows, start + ref.shape[0])
        out_ref[low - first : high - first] += ref[low - start : high - start]


def on_device(obs_minus_bg, obs_minus_an, tile_of_row, owner_order):
    n_bin = lax.axis_size("bin")
    n_cycle = lax.axis_size("cycle")
    rows, width = obs_minus_bg.shape
    tiles = owner_order.shape[0]
    per_owner = tiles // n_bin
    slots = -(-(2 * rows // tiles) // 8) * 8
    rows_c = width // n_cycle
    tile = tile_of_row.reshape(1, rows)
    padded = -(-tiles // 16) * 16
    sizes = (n_bin, per_owner, slots)
    cfg = CFG
    lanes = {"F": MID, "S": WIDE} if cfg["first"] == "M" else {"F": WIDE, "S": MID}
    places = {MID: place_mid, WIDE: place_wide}

    def slot_shapes(p):
        return [jax.ShapeDtypeStruct((slots, 2 * WIDE if lanes[p] == WIDE else CRIS_SLOT), jnp.bfloat16)] * n_bin

    *first, keys, bg, an = pl.pallas_call(
        functools.partial(first_place_kernel, places[lanes["F"]], sizes),
        out_shape=slot_shapes("F")
        + [jax.ShapeDtypeStruct((padded, rows), jnp.int32)]
        + [jax.ShapeDtypeStruct((rows, width), jnp.bfloat16)] * 2,
        in_specs=[HBM] * 4,
        out_specs=[VMEM] * (n_bin + 3),
        scratch_shapes=[
            pltpu.SMEM((tiles,), jnp.int32),
            pltpu.VMEM((1, rows), jnp.int32),
            pltpu.SemaphoreType.DMA((6,)),
        ],
        compiler_params=PARAMS,
    )(*(pltpu.with_memory_space_constraint(x, pltpu.HBM) for x in (owner_order, tile, obs_minus_bg, obs_minus_an)))
    second = pl.pallas_call(
        functools.partial(second_place_kernel, places[lanes["S"]], sizes),
        out_shape=slot_shapes("S"),
        in_specs=[VMEM] * 3,
        out_specs=[VMEM] * n_bin,
        compiler_params=PARAMS,
    )(keys, bg, an)
    owned = {"F": to_owners(first, cfg["order"]["F"]), "S": to_owners(second, cfg["order"]["S"])}

    kept = n_cycle // 8 * rows_c
    sent = kept + SUMS
    half = 2 * (sent + kept)

    def bounds(cuts, end):
        return list(zip([0, *cuts], [*cuts, end]))

    core_spans = {p: bounds(cfg["core"][p], half) for p in "FS"}
    z1_spans = {p: bounds(cfg["z1"][p], sent + kept) for p in "FS"}
    z2_spans = {p: bounds(cfg["z2"][p], sent) for p in "FS"}
    memo, busy = {}, set()

    def get(name):
        if name not in memo:
            assert name not in busy
            busy.add(name)
            memo[name] = make(*name)
            busy.discard(name)
        return memo[name]

    def after(*name):
        return [get(n) for n in cfg["after"].get(name, ())]

    def overlapping(kind, p, spans, low, high, shift=0):
        hits = [(i, start + shift) for i, (start, end) in enumerate(spans) if start + shift < high and low < end + shift]
        return [get((kind, p, i)) for i, _ in hits], [start for _, start in hits]

    def summed(p, low, high, z1, waits):
        terms, starts = overlapping("core", p, core_spans[p], low, high)
        if z1:
            more, more_starts = overlapping("z1", p, z1_spans[p], low, high, sent + kept)
            terms, starts = terms + more, starts + more_starts
        return pl.pallas_call(
            functools.partial(sum_kernel, low, starts, len(waits)),
            out_shape=jax.ShapeDtypeStruct((high - low, lanes[p]), jnp.float32),
            in_specs=[VMEM] * (1 + len(terms)) + [ANY] * len(waits),
            out_specs=VMEM,
            compiler_params=PARAMS,
        )(get(("moments", p))[-1], *terms, *waits)

    def make(kind, p, i=None):
        if kind == "moments":
            waits = after(kind, p)
            shapes = [end - start for start, end in core_spans[p]] + [half]
            return pl.pallas_call(
                functools.partial(moment_kernel, lanes[p], rows_c, n_cycle, n_bin, len(waits)),
                out_shape=[jax.ShapeDtypeStruct((size, lanes[p]), jnp.float32) for size in shapes],
                in_specs=[VMEM] * n_bin + [ANY] * len(waits),
                out_specs=[VMEM] * len(shapes),
                scratch_shapes=[pltpu.VMEM((WIDE, lanes[p]), jnp.float32)],
                compiler_params=PARAMS,
            )(*owned[p], *waits)
        if kind == "got":
            return owned[p][i]
        if kind == "core":
            return swap(get(("moments", p))[i], 1, n_cycle)
        if kind == "z1":
            low, high = z1_spans[p][i]
            return swap(summed(p, low, high, False, after(kind, p, i)), 2, n_cycle)
        if kind == "send":
            low, high = z2_spans[p][i]
            return summed(p, low + sent + kept, high + sent + kept, True, after(kind, p, i))
        if kind == "z2":
            return swap(get(("send", p, i)), 4, n_cycle)
        if kind == "keep":
            return summed(p, half - kept, half, True, after(kind, p))

    def ends(p):
        n = len(z2_spans[p])
        keep, send, got = get(("keep", p)), get(("send", p, n - 1)), [get(("z2", p, i)) for i in range(n)]
        bit = 8
        while bit < n_cycle:
            got = jnp.concatenate(got)
            part = keep.shape[0] // 2
            send = jnp.concatenate([keep[:part] + got[:part], send[-SUMS:] + got[-SUMS:]])
            keep, got = keep[part:] + got[part:-SUMS], [swap(send, bit, n_cycle)]
            bit *= 2
        return [keep, send, *got]

    wide, mid = (ends(p) for p in sorted("FS", key=lambda p: -lanes[p]))
    mid = pl.pallas_call(
        functools.partial(finish_mid_kernel, rows_c),
        out_shape=jax.ShapeDtypeStruct((rows_c, width), jnp.float32),
        in_specs=[VMEM] * len(mid),
        out_specs=VMEM,
        compiler_params=PARAMS,
    )(*mid)
    return pl.pallas_call(
        functools.partial(finish_kernel, rows_c),
        out_shape=jax.ShapeDtypeStruct((per_owner, rows_c, width), jnp.float32),
        in_specs=[VMEM] * (len(wide) + 1),
        out_specs=HBM,
        scratch_shapes=[
            pltpu.VMEM((rows_c, width), jnp.float32),
            pltpu.VMEM((rows_c, width), jnp.float32),
            pltpu.SemaphoreType.DMA((3,)),
        ],
        compiler_params=PARAMS,
    )(*wide, mid)


def solution(mesh):
    return jax.shard_map(
        on_device,
        mesh=mesh,
        in_specs=(
            P(("cycle", "bin"), None),
            P(("cycle", "bin"), None),
            P(("cycle", "bin"), None),
            P(),
        ),
        out_specs=P("bin", "cycle", None),
        check_vma=False,
    )
```
